512 devices in a mesh: space: 128 (over y, z, core), head: 4 (over x).
Axes of the slice: x: 4, y: 8, z: 8, core: 2. Of those that a mesh axis runs over, the one named last changes fastest.
Arguments:
- tokens: bfloat16 [131072, 1024], P('space', 'head'), may hold values from -6 to 6
- norm_gain: float32 [1024], replicated, may hold values from 0.25 to 1.75
- w_qkv: bfloat16 [3, 1024, 1024], P(None, None, 'head'), may hold values from -0.1875 to 0.1875
- w_out: bfloat16 [1024, 1024], P('head'), may hold values from -1 to 1
- window_id: int32 [128, 1024], P('space'), may hold values from 0 to 2, never falling along the last dimension, each value on 1 to 512 neighbouring positions
- carry: int32 [128], P('space'), may hold values from 0 to 256, as said below
Outputs:
- updated: bfloat16 [131072, 1024], P('space', 'head')
The draws below stay inside these ranges and needn't reach their ends.
Inputs may be any that keep to these rules, and one draw needn't show every extreme that they name: `carry`: the last device carries 0; some other device carries exactly 256. `window_id`: on each device labels never fall along the tokens, each of the 3 labels is used, and some window has exactly 512 tokens.
All inputs are finite; a program needn't handle non-finite values.
Results may differ from the reference program's by a relative error of at most 0.018.
Values may be sent and summed in bfloat16 or wider, within the bound.
A program may use at most 64 MiB of HBM per device.

```python
import math
import jax
import jax.numpy as jnp
import numpy as np
from jax import lax

D = 1024
HEADS = 16
HS = 64
TOK_DEV = 1024
WMAX = 512
WINS = 3
CAP = 256
TOKENS = 131072
N_SPACE = 128


def draw_carry(key, part):
    key = jax.random.fold_in(key, 11)
    counts = jax.random.randint(jax.random.fold_in(key, 1), (N_SPACE,), 1, CAP + 1).astype(jnp.int32)
    chosen = jax.random.randint(jax.random.fold_in(key, 2), (), 0, N_SPACE - 1)
    counts = counts.at[chosen].set(CAP)
    counts = counts.at[N_SPACE - 1].set(0)
    return counts.astype(jnp.int32)


def steps_of(key, extent, cuts, smallest, high):
    loudness = 1.0
    for axis_at, blocks in cuts:
        steps = jax.random.uniform(jax.random.fold_in(jax.random.fold_in(key, 6), axis_at), (blocks,), jnp.float32, smallest / len(cuts), high / len(cuts))
        loudness = loudness * jnp.repeat(jnp.exp(steps), extent[axis_at] // blocks).reshape((-1,) + (1,) * (len(extent) - 1 - axis_at))
    return loudness


def length_profile(count, total, limit, slope):
    weights = [(1 << 20) // math.isqrt(grade ** slope) + 1 for grade in range(2, count + 1)]
    rest, holding = total - limit - (count - 1), [1] * (count - 1)
    while rest > 0:
        free = [i for i in range(count - 1) if holding[i] < limit]
        whole, budget = sum([weights[i] for i in free]), rest
        for i in free:
            addition = min(limit - holding[i], max(1, budget * weights[i] // whole), rest)
            holding[i] = holding[i] + addition
            rest = rest - addition
    return np.array([limit] + holding)


def uneven_parts(own_key, count, total, most, lean):
    if count == 2:
        one = jax.random.randint(own_key, (), max(1, total - most), min(most, total - 1) + 1)
        return jnp.stack([one, total - one])
    lengths = jnp.asarray(length_profile(count, total, most, lean), jnp.int32)
    twos = (count - 1) // 2
    source_of, receiver = lengths[1:1 + 2 * twos:2], lengths[2:2 + 2 * twos:2]
    room = jnp.minimum(source_of - 1, most - receiver)
    shifted = jax.random.randint(jax.random.fold_in(own_key, 1), (twos,), 0, 1 << 20) % (room + 1)
    lengths = lengths.at[1:1 + 2 * twos:2].set(source_of - shifted).at[2:2 + 2 * twos:2].set(receiver + shifted)
    return lengths[jax.random.permutation(jax.random.fold_in(own_key, 2), count)]


def noise(own_key, extent, scale, most, pieces=(), held_as=jnp.bfloat16):
    gain = steps_of(own_key, extent, pieces, -0.22, 0.18) if pieces else 1.0
    result = jax.random.normal(own_key, extent, jnp.float32) * scale * gain
    return jnp.minimum(jnp.maximum(result, -most), most).astype(held_as)


def setup_inputs(seed: int = 0) -> dict:
    streams_of = jax.random.split(jax.random.key(seed), 7)
    tokens = noise(streams_of[0], (TOKENS, D), 1.0, 6.0, ((0, 128), (1, 4)))
    norm_gain = jnp.clip(1.0 + 0.15 * jax.random.normal(streams_of[1], (D,), jnp.float32), 0.25, 1.75)
    w_qkv = noise(streams_of[2], (3, D, D), D ** -0.5, 0.1875, ((2, 4),))
    w_out = noise(streams_of[3], (D, D), 32 ** -0.5, 1.0, ((0, 4),))
    window_id = jax.vmap(lambda own: jnp.searchsorted(jnp.cumsum(uneven_parts(own, WINS, TOK_DEV, WMAX, 2)), jnp.arange(TOK_DEV), side="right"))(jax.random.split(streams_of[4], N_SPACE)).reshape((N_SPACE, TOK_DEV)).astype(jnp.int32)
    carry = draw_carry(jax.random.fold_in(streams_of[6], 71), 0)
    return dict(tokens=tokens, norm_gain=norm_gain, w_qkv=w_qkv, w_out=w_out, window_id=window_id, carry=carry)


eps = 1e-05

def attend_all(block, labels):
    rows = block.shape[0]
    query = block[:, 0].astype(jnp.float32).reshape(rows, HEADS, HS)
    key_rows = block[:, 1].astype(jnp.float32).reshape(rows, HEADS, HS)
    value_rows = block[:, 2].astype(jnp.float32).reshape(rows, HEADS, HS)
    scores = jnp.einsum('qhd,khd->hqk', query, key_rows) * HS ** (-0.5)
    allowed = (labels[:, None] == labels[None, :]) & (labels[:, None] >= 0)
    scores = jnp.where(allowed[None], scores, -1e+30)
    probs = jax.nn.softmax(scores, axis=-1).astype(jnp.bfloat16)
    out = jnp.einsum('hqk,khd->qhd', probs.astype(jnp.float32), value_rows)
    return out.reshape(rows, D).astype(jnp.bfloat16)

def per_device(args):
    local, local_lab, incoming, incoming_lab = args
    block = jnp.concatenate([local, incoming], axis=0)
    labels = jnp.concatenate([local_lab, incoming_lab], axis=0)
    out = attend_all(block, labels)
    return (out[:TOK_DEV], out[TOK_DEV:])

def reference(tokens, norm_gain, w_qkv, w_out, window_id, carry):
    full = tokens.astype(jnp.float32)
    mean = lax.optimization_barrier(jnp.mean(full, axis=1, keepdims=True))
    var = lax.optimization_barrier(jnp.mean((full - mean) ** 2, axis=1, keepdims=True))
    normed = ((full - mean) * lax.rsqrt(var + eps) * norm_gain).astype(jnp.bfloat16)
    qkv = jnp.einsum('td,cde->tce', normed.astype(jnp.float32), w_qkv.astype(jnp.float32)).astype(jnp.bfloat16)
    qkv = qkv.reshape(N_SPACE, TOK_DEV, 3, D)
    position = jnp.arange(TOK_DEV, dtype=jnp.int32)
    moved = position[None, :] >= (TOK_DEV - carry)[:, None]
    local_lab = jnp.where(moved, -1, window_id).astype(jnp.int32)
    tail = qkv[:, TOK_DEV - CAP:]
    tail_ok = jnp.arange(CAP, dtype=jnp.int32)[None, :] >= (CAP - carry)[:, None]
    tail_lab = jnp.where(tail_ok, 0, -1).astype(jnp.int32)
    incoming = jnp.concatenate([jnp.zeros((1, CAP, 3, D), jnp.bfloat16), tail[:-1]], axis=0)
    incoming_lab = jnp.concatenate([jnp.full((1, CAP), -1, jnp.int32), tail_lab[:-1]], axis=0)
    own, back = lax.map(per_device, (qkv, local_lab, incoming, incoming_lab))
    following = jnp.concatenate([back[1:], jnp.zeros((1, CAP, D), jnp.bfloat16)], axis=0)
    padded = jnp.concatenate([jnp.zeros((N_SPACE, TOK_DEV - CAP, D), jnp.bfloat16), following], axis=1)
    attended = jnp.where(moved[:, :, None], padded, own).reshape(TOKENS, D)
    branch = jnp.dot(attended, w_out, preferred_element_type=jnp.float32)
    return (full + branch).astype(jnp.bfloat16)
```

```python
import functools
import math

import jax
import jax.numpy as jnp
from jax import lax
from jax.experimental import pallas as pl
from jax.experimental.pallas import tpu as pltpu
from jax.sharding import PartitionSpec as P

MESH = pl.DeviceIdType.MESH
F32 = jnp.float32
BF16 = jnp.bfloat16

HS = 64
CAP = 256
ROWS = 1024
ALL = ROWS + CAP
WIDTH = 256
PARTS = 4
CH = 128
NCH = ROWS // CH
BLK = 256
NBLK = ROWS // BLK
AHEAD = 3
TILE = 16
EPS = 1e-05
QSCALE = HS**-0.5 * math.log2(math.e)
NEG = -1e30


def chunk_at(i):
    return (i + NCH - CAP // CH) % NCH


def kernel(
    tok_hbm, gain_hbm, wqkv_hbm, wout_hbm, wid_hbm, carry_ref, out_any,
    gain_ref, wid_ref, xg, wq, wo, normed, qk, vv, lab, labin, bias, labcol, back, att, attin, part, hop, relay, fin,
    score, prob, outv,
    own_sem, wsem, ag_send, ag_recv, c_send, c_recv, t_send, t_recv, b_send, b_recv,
    rs_send, rs_recv, out_sem,
):
    me = lax.axis_index("head")
    spot = lax.axis_index("space")
    spots = lax.axis_size("space")
    right, left = lax.rem(me + 1, PARTS), lax.rem(me + PARTS - 1, PARTS)
    far = lax.rem(me + 2, PARTS)
    after, before = lax.rem(spot + 1, spots), lax.rem(spot + spots - 1, spots)
    to_right, to_left = {"head": right}, {"head": left}
    to_after, to_before = {"space": after}, {"space": before}

    own = pltpu.make_async_copy(tok_hbm, xg.at[me], own_sem)
    own.start()

    barrier = pltpu.get_barrier_semaphore()
    for there in (to_right, to_left, to_before):
        pl.semaphore_signal(barrier, inc=1, device_id=there, device_id_type=MESH)

    load_wid = pltpu.make_async_copy(wid_hbm, wid_ref, wsem.at[2])
    load_wid.start()
    load_gain = pltpu.make_async_copy(gain_hbm, gain_ref, wsem.at[3])
    load_gain.start()
    load_wq = pltpu.make_async_copy(wqkv_hbm, wq, wsem.at[0])
    load_wq.start()
    load_wo = pltpu.make_async_copy(wout_hbm, wo, wsem.at[1])
    load_wo.start()

    count = carry_ref[0]
    lab[...] = jnp.full(lab.shape, count, jnp.int32).astype(F32)
    own.wait()
    pl.semaphore_wait(barrier, 3)

    def remote(src, dst, send, recv, there):
        return pltpu.make_async_remote_copy(
            src_ref=src, dst_ref=dst, send_sem=send, recv_sem=recv, device_id=there, device_id_type=MESH
        )

    def gather_copy(kind, i):
        rows = chunk_at(i) * CH
        slot, start, size, there = (
            (me, rows, CH, to_right),
            (me, rows, CH, to_left),
            (left, rows, CH // 2, to_right),
            (right, rows + CH // 2, CH // 2, to_left),
        )[kind]
        view = xg.at[slot, pl.ds(pl.multiple_of(start, CH // 2), size), :]
        return remote(view, view, ag_send.at[kind, i], ag_recv.at[kind, i], there)

    def gather_wait(kind, i):
        rows = chunk_at(i) * CH
        slot, start, size = (
            (left, rows, CH),
            (right, rows, CH),
            (far, rows, CH // 2),
            (far, rows + CH // 2, CH // 2),
        )[kind]
        view = xg.at[slot, pl.ds(pl.multiple_of(start, CH // 2), size), :]
        remote(view, view, ag_send.at[kind, i], ag_recv.at[kind, i], to_right).wait_recv()

    for i in range(AHEAD):
        gather_copy(0, i).start()
        gather_copy(1, i).start()
    code = remote(lab, labin, c_send, c_recv, to_after)
    code.start()

    vv[:, :, CH:] = jnp.ones((2, ALL, CH), BF16)

    def columns_of(queries, first):
        for k in range(queries.shape[1] // CH):
            piece = jnp.broadcast_to(queries[0:1, k * CH : (k + 1) * CH], (CH, CH))
            labcol[first + k * CH : first + (k + 1) * CH, :] = piece.T

    def allow(block, queries, first, start, stop):
        keys = jnp.where(queries < 0.0, -2.0, queries)
        rows = slice(block * BLK, (block + 1) * BLK)
        column = labcol[rows, :]
        for k in range(start, stop, CH):
            bias[rows, k : k + CH] = jnp.where(column == keys[0:1, k - first : k - first + CH], 0.0, NEG)

    def labels_here():
        spread = jnp.broadcast_to(wid_ref[...].astype(F32), (8, ROWS))
        place = lax.broadcasted_iota(jnp.int32, (8, ROWS), 1)
        return jnp.where(place >= ROWS - count, -1.0, spread)

    bands = {0: (0, 768), 1: (0, 1024), 2: (0, 1280), 3: (256, 1024), 4: (512, 768)}
    load_wid.wait()
    mine = labels_here()
    columns_of(mine, CAP)
    for block in range(1, NBLK + 1):
        first, extent = bands[block]
        allow(block, mine, CAP, max(first, CAP), first + extent)

    def admit():
        code.wait_recv()
        place = lax.broadcasted_iota(jnp.int32, (8, CAP), 1).astype(F32)
        theirs = jnp.where(place >= CAP - labin[0:1, 0:1], 0.0, -1.0)
        columns_of(theirs, 0)
        for block in range(3):
            allow(block, theirs, 0, 0, CAP)
        allow(0, labels_here(), CAP, CAP, 768)

    load_gain.wait()
    load_wq.wait()
    gain = gain_ref[...]

    def project(i):
        gather_wait(2, i)
        gather_wait(3, i)
        rows = pl.multiple_of(chunk_at(i) * CH, CH)
        for r in range(0, CH, TILE):
            slices = [
                xg[p, pl.ds(pl.multiple_of(rows + r, TILE), TILE), :].astype(F32) for p in range(PARTS)
            ]
            mean = jnp.sum(sum(slices), axis=1, keepdims=True) * (1.0 / (PARTS * WIDTH))
            centred = [x - mean for x in slices]
            var = jnp.sum(sum(x * x for x in centred), axis=1, keepdims=True) * (1.0 / (PARTS * WIDTH))
            rstd = lax.rsqrt(var + EPS)
            for p in range(PARTS):
                cols = slice(p * WIDTH, (p + 1) * WIDTH)
                normed[r : r + TILE, cols] = (centred[p] * rstd * gain[:, cols]).astype(BF16)
        here = pl.ds(pl.multiple_of(rows + CAP, CH), CH)
        x = normed[...]
        qk[0, here, :] = (jnp.dot(x, wq[0], preferred_element_type=F32) * QSCALE).astype(BF16)
        qk[1, here, :] = jnp.dot(x, wq[1], preferred_element_type=F32).astype(BF16)
        v = jnp.dot(x, wq[2], preferred_element_type=F32).astype(BF16)
        vv[0, here, 0:128] = v[:, 0:128]
        vv[1, here, 0:128] = v[:, 128:256]

    tail_qk = remote(qk.at[:, pl.ds(ROWS, CAP), :], qk.at[:, pl.ds(0, CAP), :], t_send.at[0], t_recv.at[0], to_after)
    tail_v = remote(
        vv.at[:, pl.ds(ROWS, CAP), pl.ds(0, 128)], vv.at[:, pl.ds(0, CAP), pl.ds(0, 128)],
        t_send.at[1], t_recv.at[1], to_after,
    )

    def arrive(i):
        gather_wait(0, i)
        gather_wait(1, i)
        gather_copy(2, i).start()
        gather_copy(3, i).start()

    def more(i):
        gather_copy(0, i).start()
        gather_copy(1, i).start()

    arrive(0)
    more(AHEAD)

    def gather_step(i, _):
        arrive(i)

        @pl.when(i + AHEAD < NCH)
        def _():
            more(i + AHEAD)

        project(i - 1)

        @pl.when(i == 2)
        def _():
            tail_qk.start()
            tail_v.start()

        return 0

    lax.fori_loop(1, NCH - 1, gather_step, 0)
    arrive(NCH - 1)

    lanes = lax.broadcasted_iota(jnp.int32, (1, 128), 1) < HS

    def attend(block, target):
        first, extent = bands[block]
        rows = slice(block * BLK, (block + 1) * BLK)
        span = slice(first, first + extent)

        def pair_step(pair, _):
            cols = pl.ds(pl.multiple_of(pair * 128, 128), 128)
            q = qk[0, rows, cols]
            for half in range(2):
                q_half = jnp.where(lanes if half == 0 else ~lanes, q, jnp.zeros_like(q))
                for k in range(0, extent, BLK):
                    score[half, :, k : k + BLK] = lax.dot_general(
                        q_half, qk[1, first + k : first + k + BLK, cols], (((1,), (1,)), ((), ())),
                        preferred_element_type=F32,
                    )
            results = []
            for half in range(2):
                for r in range(0, BLK, TILE):
                    allowed = score[half, r : r + TILE, 0:extent] + bias[block * BLK + r : block * BLK + r + TILE, span]
                    top = jnp.max(allowed, axis=1, keepdims=True)
                    prob[half, r : r + TILE, 0:extent] = jnp.exp2(allowed - top).astype(BF16)
                out = jnp.dot(prob[half, :, 0:extent], vv[pair, span, :], preferred_element_type=F32)
                results.append(out[:, 0:128] / out[:, 128:256])
            target[:, cols] = jnp.where(lanes, results[0], results[1]).astype(BF16)
            return 0

        lax.fori_loop(0, 2, pair_step, 0)

    project(NCH - 2)
    project(NCH - 1)
    load_wo.wait()
    give_back = remote(attin, back, b_send, b_recv, to_before)

    half = BLK // 2
    low, high = pl.ds(0, half), pl.ds(half, half)

    def rs_copy(kind, b):
        src, dst, there = (
            (part.at[b, far, low, :], hop.at[b, 0], to_right),
            (part.at[b, far, high, :], hop.at[b, 1], to_left),
            (part.at[b, right, high, :], fin.at[b, 0, high, :], to_right),
            (part.at[b, left, low, :], fin.at[b, 1, low, :], to_left),
            (relay.at[b, 0], fin.at[b, 0, low, :], to_right),
            (relay.at[b, 1], fin.at[b, 1, high, :], to_left),
        )[kind]
        return remote(src, dst, rs_send.at[kind, b], rs_recv.at[kind, b], there)

    def pass_on(b):
        rs_copy(0, b).wait_recv()
        relay[b, 0] = (hop[b, 0].astype(F32) + part[b, right, low, :].astype(F32)).astype(BF16)
        rs_copy(4, b).start()
        rs_copy(1, b).wait_recv()
        relay[b, 1] = (hop[b, 1].astype(F32) + part[b, left, high, :].astype(F32)).astype(BF16)
        rs_copy(5, b).start()

    order = (2, 0, 1, 3)
    for step, b in enumerate(order):
        if step == 1:
            admit()
            tail_qk.wait_recv()
            tail_v.wait_recv()
            attend(0, attin)
            give_back.start()
        attend(b + 1, att)
        if b == NBLK - 1:
            give_back.wait_recv()
            moved = labcol[ALL - BLK : ALL, :] < 0.0
            for cols in (slice(0, 128), slice(128, 256)):
                att[:, cols] = jnp.where(moved, back[:, cols].astype(F32), att[:, cols].astype(F32)).astype(BF16)
        rows = att[...]
        for p in range(PARTS):
            part[b, p] = jnp.dot(
                rows, wo[:, p * WIDTH : (p + 1) * WIDTH], preferred_element_type=F32
            ).astype(BF16)
        for kind in range(4):
            rs_copy(kind, b).start()
        if step >= 1:
            pass_on(order[step - 1])
    pass_on(order[-1])

    def store_out(b):
        rows = pl.ds(b * BLK, BLK)
        return pltpu.make_async_copy(outv.at[rows, :], out_any.at[rows, :], out_sem.at[b])

    def finish(b):
        for kind in range(2, 6):
            rs_copy(kind, b).wait_recv()
        rows = slice(b * BLK, (b + 1) * BLK)
        outv[rows, :] = (
            xg[me, rows, :].astype(F32)
            + part[b, me].astype(F32)
            + fin[b, 0].astype(F32)
            + fin[b, 1].astype(F32)
        ).astype(BF16)

    for b in order:
        finish(b)
        store_out(b).start()

    def drain(i, _):
        for kind in range(4):
            gather_copy(kind, i).wait_send()
        return 0

    lax.fori_loop(0, NCH, drain, 0)
    code.wait_send()
    tail_qk.wait_send()
    tail_v.wait_send()
    give_back.wait_send()
    for b in range(NBLK):
        for kind in range(6):
            rs_copy(kind, b).wait_send()
        store_out(b).wait()


def local(tokens, norm_gain, w_qkv, w_out, window_id, carry):
    there = pl.BlockSpec(memory_space=pltpu.HBM)
    dma = pltpu.SemaphoreType.DMA
    return pl.pallas_call(
        kernel,
        out_shape=jax.ShapeDtypeStruct(tokens.shape, BF16),
        in_specs=[there] * 5 + [pl.BlockSpec(memory_space=pltpu.SMEM)],
        out_specs=pl.BlockSpec(memory_space=pl.ANY),
        scratch_shapes=[
            pltpu.VMEM((1, PARTS * WIDTH), F32),
            pltpu.VMEM((1, ROWS), jnp.int32),
            pltpu.VMEM((PARTS, ROWS, WIDTH), BF16),
            pltpu.VMEM((3, PARTS * WIDTH, WIDTH), BF16),
            pltpu.VMEM((WIDTH, PARTS * WIDTH), BF16),
            pltpu.VMEM((CH, PARTS * WIDTH), BF16),
            pltpu.VMEM((2, ALL, WIDTH), BF16),
            pltpu.VMEM((2, ALL, WIDTH), BF16),
            pltpu.VMEM((8, 128), F32),
            pltpu.VMEM((8, 128), F32),
            pltpu.VMEM((ALL, ALL), F32),
            pltpu.VMEM((ALL, 128), F32),
            pltpu.VMEM((CAP, WIDTH), BF16),
            pltpu.VMEM((BLK, WIDTH), BF16),
            pltpu.VMEM((CAP, WIDTH), BF16),
            pltpu.VMEM((NBLK, PARTS, BLK, WIDTH), BF16),
            pltpu.VMEM((NBLK, 2, BLK // 2, WIDTH), BF16),
            pltpu.VMEM((NBLK, 2, BLK // 2, WIDTH), BF16),
            pltpu.VMEM((NBLK, 2, BLK, WIDTH), BF16),
            pltpu.VMEM((2, BLK, ALL), F32),
            pltpu.VMEM((2, BLK, ALL), BF16),
            pltpu.VMEM((ROWS, WIDTH), BF16),
            dma,
            dma((4,)),
            dma((4, NCH)),
            dma((4, NCH)),
            dma,
            dma,
            dma((2,)),
            dma((2,)),
            dma,
            dma,
            dma((6, NBLK)),
            dma((6, NBLK)),
            dma((NBLK,)),
        ],
        compiler_params=pltpu.CompilerParams(
            collective_id=0, has_side_effects=True, vmem_limit_bytes=56 * 1024 * 1024
        ),
        cost_estimate=pl.CostEstimate(flops=4_000_000_000, bytes_accessed=4_000_000, transcendentals=5_000_000),
    )(tokens, norm_gain.reshape(1, PARTS * WIDTH), w_qkv, w_out, window_id, carry)


def solution(mesh):
    return jax.shard_map(
        local,
        mesh=mesh,
        in_specs=(
            P("space", "head"),
            P(),
            P(None, None, "head"),
            P("head", None),
            P("space", None),
            P("space"),
        ),
        out_specs=P("space", "head"),
        check_vma=False,
    )
```

```python
import functools
import math

import jax
import jax.numpy as jnp
from jax import lax
from jax.experimental import pallas as pl
from jax.experimental.pallas import tpu as pltpu
from jax.sharding import PartitionSpec as P

MESH = pl.DeviceIdType.MESH
F32 = jnp.float32
BF16 = jnp.bfloat16

HS = 64
CAP = 256
ROWS = 1024
ALL = ROWS + CAP
WIDTH = 256
PARTS = 4
CH = 128
NCH = ROWS // CH
BLK = 256
NBLK = ROWS // BLK
AHEAD = 3
TILE = 16
EPS = 1e-05
QSCALE = HS**-0.5 * math.log2(math.e)
NEG = -1e30


def chunk_at(i):
    return NCH - 2 - 2 * (i // 2) + i % 2


def kernel(
    tok_hbm, gain_hbm, wqkv_hbm, wout_hbm, wid_hbm, carry_ref, out_any,
    gain_ref, wid_ref, xg, wq, wo, normed, qk, vv, lab, labin, bias, labcol, back, att, attin, part, hop, relay, fin,
    score, prob, outv, held, top_held, shrink,
    own_sem, wsem, ag_send, ag_recv, c_send, c_recv, t_send, t_recv, b_send, b_recv,
    rs_send, rs_recv, out_sem,
):
    me = lax.axis_index("head")
    spot = lax.axis_index("space")
    spots = lax.axis_size("space")
    right, left = lax.rem(me + 1, PARTS), lax.rem(me + PARTS - 1, PARTS)
    far = lax.rem(me + 2, PARTS)
    after, before = lax.rem(spot + 1, spots), lax.rem(spot + spots - 1, spots)
    to_right, to_left = {"head": right}, {"head": left}
    to_after, to_before = {"space": after}, {"space": before}

    own = pltpu.make_async_copy(tok_hbm, xg.at[me], own_sem)
    own.start()

    barrier = pltpu.get_barrier_semaphore()
    for there in (to_right, to_left, to_before):
        pl.semaphore_signal(barrier, inc=1, device_id=there, device_id_type=MESH)

    load_wid = pltpu.make_async_copy(wid_hbm, wid_ref, wsem.at[2])
    load_wid.start()
    load_gain = pltpu.make_async_copy(gain_hbm, gain_ref, wsem.at[3])
    load_gain.start()
    load_wq = pltpu.make_async_copy(wqkv_hbm, wq, wsem.at[0])
    load_wq.start()
    load_wo = pltpu.make_async_copy(wout_hbm, wo, wsem.at[1])
    load_wo.start()

    count = carry_ref[0]
    lab[...] = jnp.full(lab.shape, count, jnp.int32).astype(F32)
    own.wait()
    pl.semaphore_wait(barrier, 3)

    def remote(src, dst, send, recv, there):
        return pltpu.make_async_remote_copy(
            src_ref=src, dst_ref=dst, send_sem=send, recv_sem=recv, device_id=there, device_id_type=MESH
        )

    def gather_copy(kind, i):
        rows = chunk_at(i) * CH
        slot, start, size, there = (
            (me, rows, CH, to_right),
            (me, rows, CH, to_left),
            (left, rows, CH // 2, to_right),
            (right, rows + CH // 2, CH // 2, to_left),
        )[kind]
        view = xg.at[slot, pl.ds(pl.multiple_of(start, CH // 2), size), :]
        return remote(view, view, ag_send.at[kind, i], ag_recv.at[kind, i], there)

    def gather_wait(kind, i):
        rows = chunk_at(i) * CH
        slot, start, size = (
            (left, rows, CH),
            (right, rows, CH),
            (far, rows, CH // 2),
            (far, rows + CH // 2, CH // 2),
        )[kind]
        view = xg.at[slot, pl.ds(pl.multiple_of(start, CH // 2), size), :]
        remote(view, view, ag_send.at[kind, i], ag_recv.at[kind, i], to_right).wait_recv()

    for i in range(AHEAD):
        gather_copy(0, i).start()
        gather_copy(1, i).start()
    code = remote(lab, labin, c_send, c_recv, to_after)
    code.start()

    vv[:, :, CH:] = jnp.ones((2, ALL, CH), BF16)

    def columns_of(queries, first):
        for k in range(queries.shape[1] // CH):
            piece = jnp.broadcast_to(queries[0:1, k * CH : (k + 1) * CH], (CH, CH))
            labcol[first + k * CH : first + (k + 1) * CH, :] = piece.T

    def allow(block, queries, first, start, stop):
        keys = jnp.where(queries < 0.0, -2.0, queries)
        rows = slice(block * BLK, (block + 1) * BLK)
        column = labcol[rows, :]
        for k in range(start, stop, CH):
            bias[rows, k : k + CH] = jnp.where(column == keys[0:1, k - first : k - first + CH], 0.0, NEG)

    def labels_here():
        spread = jnp.broadcast_to(wid_ref[...].astype(F32), (8, ROWS))
        place = lax.broadcasted_iota(jnp.int32, (8, ROWS), 1)
        return jnp.where(place >= ROWS - count, -1.0, spread)

    bands = {0: (0, 768), 1: (0, 1024), 2: (0, 1280), 3: (256, 1024), 4: (512, 768)}
    load_wid.wait()
    mine = labels_here()
    columns_of(mine, CAP)
    for block in range(1, NBLK + 1):
        first, extent = bands[block]
        allow(block, mine, CAP, max(first, CAP), first + extent)

    def admit():
        code.wait_recv()
        place = lax.broadcasted_iota(jnp.int32, (8, CAP), 1).astype(F32)
        theirs = jnp.where(place >= CAP - labin[0:1, 0:1], 0.0, -1.0)
        columns_of(theirs, 0)
        for block in range(3):
            allow(block, theirs, 0, 0, CAP)
        allow(0, labels_here(), CAP, CAP, 768)

    load_gain.wait()
    load_wq.wait()
    gain = gain_ref[...]

    def project(i):
        gather_wait(2, i)
        gather_wait(3, i)
        rows = pl.multiple_of(chunk_at(i) * CH, CH)
        for r in range(0, CH, TILE):
            slices = [
                xg[p, pl.ds(pl.multiple_of(rows + r, TILE), TILE), :].astype(F32) for p in range(PARTS)
            ]
            mean = jnp.sum(sum(slices), axis=1, keepdims=True) * (1.0 / (PARTS * WIDTH))
            centred = [x - mean for x in slices]
            var = jnp.sum(sum(x * x for x in centred), axis=1, keepdims=True) * (1.0 / (PARTS * WIDTH))
            rstd = lax.rsqrt(var + EPS)
            for p in range(PARTS):
                cols = slice(p * WIDTH, (p + 1) * WIDTH)
                normed[r : r + TILE, cols] = (centred[p] * rstd * gain[:, cols]).astype(BF16)
        here = pl.ds(pl.multiple_of(rows + CAP, CH), CH)
        x = normed[...]
        qk[0, here, :] = (jnp.dot(x, wq[0], preferred_element_type=F32) * QSCALE).astype(BF16)
        qk[1, here, :] = jnp.dot(x, wq[1], preferred_element_type=F32).astype(BF16)
        v = jnp.dot(x, wq[2], preferred_element_type=F32).astype(BF16)
        vv[0, here, 0:128] = v[:, 0:128]
        vv[1, here, 0:128] = v[:, 128:256]

    tail_qk = remote(qk.at[:, pl.ds(ROWS, CAP), :], qk.at[:, pl.ds(0, CAP), :], t_send.at[0], t_recv.at[0], to_after)
    tail_v = remote(
        vv.at[:, pl.ds(ROWS, CAP), pl.ds(0, 128)], vv.at[:, pl.ds(0, CAP), pl.ds(0, 128)],
        t_send.at[1], t_recv.at[1], to_after,
    )

    def arrive(i):
        gather_wait(0, i)
        gather_wait(1, i)
        gather_copy(2, i).start()
        gather_copy(3, i).start()

    def more(i):
        gather_copy(0, i).start()
        gather_copy(1, i).start()

    arrive(0)
    more(AHEAD)

    def gather_step(i, _):
        arrive(i)

        @pl.when(i + AHEAD < NCH)
        def _():
            more(i + AHEAD)

        project(i - 1)

        @pl.when(i == 2)
        def _():
            tail_qk.start()
            tail_v.start()

        return 0

    lax.fori_loop(1, NCH - 1, gather_step, 0)

    lanes = lax.broadcasted_iota(jnp.int32, (1, 128), 1) < HS

    def attend(block, target, part=None, span=None):
        first, extent = bands[block] if span is None else span
        rows = slice(block * BLK, (block + 1) * BLK)
        span = slice(first, first + extent)

        def pair_step(pair, _):
            cols = pl.ds(pl.multiple_of(pair * 128, 128), 128)
            q = qk[0, rows, cols]
            for half in range(2):
                q_half = jnp.where(lanes if half == 0 else ~lanes, q, jnp.zeros_like(q))
                for k in range(0, extent, BLK):
                    score[half, :, k : k + BLK] = lax.dot_general(
                        q_half, qk[1, first + k : first + k + BLK, cols], (((1,), (1,)), ((), ())),
                        preferred_element_type=F32,
                    )
            results = []
            for half in range(2):
                for r in range(0, BLK, TILE):
                    tile = slice(r, r + TILE)
                    allowed = score[half, tile, 0:extent] + bias[block * BLK + r : block * BLK + r + TILE, span]
                    top = jnp.max(allowed, axis=1, keepdims=True)
                    if part == 0:
                        top_held[pair, half, tile, :] = jnp.broadcast_to(top, (TILE, 128))
                    elif part == 1:
                        old = top_held[pair, half, tile, :]
                        top = jnp.maximum(old[:, 0:1], top)
                        shrink[half, tile, :] = jnp.exp2(old - top)
                    prob[half, tile, 0:extent] = jnp.exp2(allowed - top).astype(BF16)
                results.append(jnp.dot(prob[half, :, 0:extent], vv[pair, span, :], preferred_element_type=F32))
            total = jnp.where(lanes, results[0][:, 0:128], results[1][:, 0:128])
            weight = jnp.where(lanes, results[0][:, 128:256], results[1][:, 128:256])
            if part == 0:
                held[pair, 0] = total
                held[pair, 1] = weight
            else:
                if part == 1:
                    scale = jnp.where(lanes, shrink[0], shrink[1])
                    total = total + scale * held[pair, 0]
                    weight = weight + scale * held[pair, 1]
                target[:, cols] = (total / weight).astype(BF16)
            return 0

        lax.fori_loop(0, 2, pair_step, 0)

    attend(3, att, 0, (512, 768))
    arrive(NCH - 1)
    project(NCH - 2)
    project(NCH - 1)
    load_wo.wait()
    give_back = remote(attin, back, b_send, b_recv, to_before)

    half = BLK // 2
    low, high = pl.ds(0, half), pl.ds(half, half)

    def rs_copy(kind, b):
        src, dst, there = (
            (part.at[b, far, low, :], hop.at[b, 0], to_right),
            (part.at[b, far, high, :], hop.at[b, 1], to_left),
            (part.at[b, right, high, :], fin.at[b, 0, high, :], to_right),
            (part.at[b, left, low, :], fin.at[b, 1, low, :], to_left),
            (relay.at[b, 0], fin.at[b, 0, low, :], to_right),
            (relay.at[b, 1], fin.at[b, 1, high, :], to_left),
        )[kind]
        return remote(src, dst, rs_send.at[kind, b], rs_recv.at[kind, b], there)

    def pass_on(b):
        rs_copy(0, b).wait_recv()
        relay[b, 0] = (hop[b, 0].astype(F32) + part[b, right, low, :].astype(F32)).astype(BF16)
        rs_copy(4, b).start()
        rs_copy(1, b).wait_recv()
        relay[b, 1] = (hop[b, 1].astype(F32) + part[b, left, high, :].astype(F32)).astype(BF16)
        rs_copy(5, b).start()

    order = (2, 1, 0, 3)
    for step, b in enumerate(order):
        if step == 0:
            attend(3, att, 1, (256, 256))
        elif step == 1:
            admit()
            tail_qk.wait_recv()
            tail_v.wait_recv()
            attend(2, att)
        elif step == 2:
            attend(0, attin)
            give_back.start()
            attend(1, att)
        else:
            attend(4, att)
            give_back.wait_recv()
            moved = labcol[ALL - BLK : ALL, :] < 0.0
            for cols in (slice(0, 128), slice(128, 256)):
                att[:, cols] = jnp.where(moved, back[:, cols].astype(F32), att[:, cols].astype(F32)).astype(BF16)
        rows = att[...]
        for p in range(PARTS):
            part[b, p] = jnp.dot(
                rows, wo[:, p * WIDTH : (p + 1) * WIDTH], preferred_element_type=F32
            ).astype(BF16)
        for kind in range(4):
            rs_copy(kind, b).start()
        if step >= 1:
            pass_on(order[step - 1])

    def store_out(b):
        rows = pl.ds(b * BLK, BLK)
        return pltpu.make_async_copy(outv.at[rows, :], out_any.at[rows, :], out_sem.at[b])

    def finish(b):
        for kind in range(2, 6):
            rs_copy(kind, b).wait_recv()
        rows = slice(b * BLK, (b + 1) * BLK)
        outv[rows, :] = (
            xg[me, rows, :].astype(F32)
            + part[b, me].astype(F32)
            + fin[b, 0].astype(F32)
            + fin[b, 1].astype(F32)
        ).astype(BF16)
        store_out(b).start()

    finish(order[0])
    finish(order[1])
    pass_on(order[3])
    finish(order[2])
    finish(order[3])

    def drain(i, _):
        for kind in range(4):
            gather_copy(kind, i).wait_send()
        return 0

    lax.fori_loop(0, NCH, drain, 0)
    code.wait_send()
    tail_qk.wait_send()
    tail_v.wait_send()
    give_back.wait_send()
    for b in range(NBLK):
        for kind in range(6):
            rs_copy(kind, b).wait_send()
        store_out(b).wait()


def local(tokens, norm_gain, w_qkv, w_out, window_id, carry):
    there = pl.BlockSpec(memory_space=pltpu.HBM)
    dma = pltpu.SemaphoreType.DMA
    return pl.pallas_call(
        kernel,
        out_shape=jax.ShapeDtypeStruct(tokens.shape, BF16),
        in_specs=[there] * 5 + [pl.BlockSpec(memory_space=pltpu.SMEM)],
        out_specs=pl.BlockSpec(memory_space=pl.ANY),
        scratch_shapes=[
            pltpu.VMEM((1, PARTS * WIDTH), F32),
            pltpu.VMEM((1, ROWS), jnp.int32),
            pltpu.VMEM((PARTS, ROWS, WIDTH), BF16),
            pltpu.VMEM((3, PARTS * WIDTH, WIDTH), BF16),
            pltpu.VMEM((WIDTH, PARTS * WIDTH), BF16),
            pltpu.VMEM((CH, PARTS * WIDTH), BF16),
            pltpu.VMEM((2, ALL, WIDTH), BF16),
            pltpu.VMEM((2, ALL, WIDTH), BF16),
            pltpu.VMEM((8, 128), F32),
            pltpu.VMEM((8, 128), F32),
            pltpu.VMEM((ALL, ALL), F32),
            pltpu.VMEM((ALL, 128), F32),
            pltpu.VMEM((CAP, WIDTH), BF16),
            pltpu.VMEM((BLK, WIDTH), BF16),
            pltpu.VMEM((CAP, WIDTH), BF16),
            pltpu.VMEM((NBLK, PARTS, BLK, WIDTH), BF16),
            pltpu.VMEM((NBLK, 2, BLK // 2, WIDTH), BF16),
            pltpu.VMEM((NBLK, 2, BLK // 2, WIDTH), BF16),
            pltpu.VMEM((NBLK, 2, BLK, WIDTH), BF16),
            pltpu.VMEM((2, BLK, ALL), F32),
            pltpu.VMEM((2, BLK, ALL), BF16),
            pltpu.VMEM((ROWS, WIDTH), BF16),
            pltpu.VMEM((2, 2, BLK, 128), F32),
            pltpu.VMEM((2, 2, BLK, 128), F32),
            pltpu.VMEM((2, BLK, 128), F32),
            dma,
            dma((4,)),
            dma((4, NCH)),
            dma((4, NCH)),
            dma,
            dma,
            dma((2,)),
            dma((2,)),
            dma,
            dma,
            dma((6, NBLK)),
            dma((6, NBLK)),
            dma((NBLK,)),
        ],
        compiler_params=pltpu.CompilerParams(
            collective_id=0, has_side_effects=True, vmem_limit_bytes=56 * 1024 * 1024
        ),
        cost_estimate=pl.CostEstimate(flops=4_000_000_000, bytes_accessed=4_000_000, transcendentals=5_000_000),
    )(tokens, norm_gain.reshape(1, PARTS * WIDTH), w_qkv, w_out, window_id, carry)


def solution(mesh):
    return jax.shard_map(
        local,
        mesh=mesh,
        in_specs=(
            P("space", "head"),
            P(),
            P(None, None, "head"),
            P("head", None),
            P("space", None),
            P("space"),
        ),
        out_specs=P("space", "head"),
        check_vma=False,
    )
```

```python
import functools
import math

import jax
import jax.numpy as jnp
from jax import lax
from jax.experimental import pallas as pl
from jax.experimental.pallas import tpu as pltpu
from jax.sharding import PartitionSpec as P

MESH = pl.DeviceIdType.MESH
F32 = jnp.float32
BF16 = jnp.bfloat16

HS = 64
CAP = 256
ROWS = 1024
ALL = ROWS + CAP
WIDTH = 256
PARTS = 4
CH = 256
LANE = 128
NCH = ROWS // CH
BLK = 256
NBLK = ROWS // BLK
AHEAD = 2
TILE = 16
EPS = 1e-05
QSCALE = HS**-0.5 * math.log2(math.e)
NEG = -1e30


def chunk_at(i):
    return NCH - 1 - i


def kernel(
    tok_hbm, gain_hbm, wqkv_hbm, wout_hbm, wid_hbm, carry_ref, out_any,
    gain_ref, wid_ref, xg, wq, wo, normed, qk, vv, lab, labin, bias, labcol, back, att, attin, part, hop, relay, fin,
    score, prob, outv, held, top_held, shrink,
    own_sem, wsem, ag_send, ag_recv, c_send, c_recv, t_send, t_recv, b_send, b_recv,
    rs_send, rs_recv, out_sem,
):
    me = lax.axis_index("head")
    spot = lax.axis_index("space")
    spots = lax.axis_size("space")
    right, left = lax.rem(me + 1, PARTS), lax.rem(me + PARTS - 1, PARTS)
    far = lax.rem(me + 2, PARTS)
    after, before = lax.rem(spot + 1, spots), lax.rem(spot + spots - 1, spots)
    to_right, to_left = {"head": right}, {"head": left}
    to_after, to_before = {"space": after}, {"space": before}

    own = pltpu.make_async_copy(tok_hbm, xg.at[me], own_sem)
    own.start()

    barrier = pltpu.get_barrier_semaphore()
    for there in (to_right, to_left, to_before):
        pl.semaphore_signal(barrier, inc=1, device_id=there, device_id_type=MESH)

    load_wid = pltpu.make_async_copy(wid_hbm, wid_ref, wsem.at[2])
    load_wid.start()
    load_gain = pltpu.make_async_copy(gain_hbm, gain_ref, wsem.at[3])
    load_gain.start()
    load_wq = pltpu.make_async_copy(wqkv_hbm, wq, wsem.at[0])
    load_wq.start()
    load_wo = pltpu.make_async_copy(wout_hbm, wo, wsem.at[1])
    load_wo.start()

    count = carry_ref[0]
    lab[...] = jnp.full(lab.shape, count, jnp.int32).astype(F32)
    own.wait()
    pl.semaphore_wait(barrier, 3)

    def remote(src, dst, send, recv, there):
        return pltpu.make_async_remote_copy(
            src_ref=src, dst_ref=dst, send_sem=send, recv_sem=recv, device_id=there, device_id_type=MESH
        )

    def gather_copy(kind, i):
        rows = chunk_at(i) * CH
        slot, start, size, there = (
            (me, rows, CH, to_right),
            (me, rows, CH, to_left),
            (left, rows, CH // 2, to_right),
            (right, rows + CH // 2, CH // 2, to_left),
        )[kind]
        view = xg.at[slot, pl.ds(pl.multiple_of(start, CH // 2), size), :]
        return remote(view, view, ag_send.at[kind, i], ag_recv.at[kind, i], there)

    def gather_wait(kind, i):
        rows = chunk_at(i) * CH
        slot, start, size = (
            (left, rows, CH),
            (right, rows, CH),
            (far, rows, CH // 2),
            (far, rows + CH // 2, CH // 2),
        )[kind]
        view = xg.at[slot, pl.ds(pl.multiple_of(start, CH // 2), size), :]
        remote(view, view, ag_send.at[kind, i], ag_recv.at[kind, i], to_right).wait_recv()

    for i in range(AHEAD):
        gather_copy(0, i).start()
        gather_copy(1, i).start()
    code = remote(lab, labin, c_send, c_recv, to_after)
    code.start()

    vv[:, :, LANE:] = jnp.ones((2, ALL, LANE), BF16)

    def columns_of(queries, first):
        for k in range(queries.shape[1] // LANE):
            piece = jnp.broadcast_to(queries[0:1, k * LANE : (k + 1) * LANE], (LANE, LANE))
            labcol[first + k * LANE : first + (k + 1) * LANE, :] = piece.T

    def allow(block, queries, first, start, stop):
        keys = jnp.where(queries < 0.0, -2.0, queries)
        rows = slice(block * BLK, (block + 1) * BLK)
        column = labcol[rows, :]
        for k in range(start, stop, LANE):
            bias[rows, k : k + LANE] = jnp.where(column == keys[0:1, k - first : k - first + LANE], 0.0, NEG)

    def labels_here():
        spread = jnp.broadcast_to(wid_ref[...].astype(F32), (8, ROWS))
        place = lax.broadcasted_iota(jnp.int32, (8, ROWS), 1)
        return jnp.where(place >= ROWS - count, -1.0, spread)

    bands = {0: (0, 768), 1: (0, 1024), 2: (0, 1280), 3: (256, 1024), 4: (512, 768)}
    load_wid.wait()
    mine = labels_here()
    columns_of(mine, CAP)
    for block in range(1, NBLK + 1):
        first, extent = bands[block]
        allow(block, mine, CAP, max(first, CAP), first + extent)

    def admit():
        code.wait_recv()
        place = lax.broadcasted_iota(jnp.int32, (8, CAP), 1).astype(F32)
        theirs = jnp.where(place >= CAP - labin[0:1, 0:1], 0.0, -1.0)
        columns_of(theirs, 0)
        for block in range(3):
            allow(block, theirs, 0, 0, CAP)
        allow(0, labels_here(), CAP, CAP, 768)

    load_gain.wait()
    load_wq.wait()
    gain = gain_ref[...]

    def project(i):
        gather_wait(2, i)
        gather_wait(3, i)
        rows = pl.multiple_of(chunk_at(i) * CH, CH)
        for r in range(0, CH, TILE):
            slices = [
                xg[p, pl.ds(pl.multiple_of(rows + r, TILE), TILE), :].astype(F32) for p in range(PARTS)
            ]
            mean = jnp.sum(sum(slices), axis=1, keepdims=True) * (1.0 / (PARTS * WIDTH))
            centred = [x - mean for x in slices]
            var = jnp.sum(sum(x * x for x in centred), axis=1, keepdims=True) * (1.0 / (PARTS * WIDTH))
            rstd = lax.rsqrt(var + EPS)
            for p in range(PARTS):
                cols = slice(p * WIDTH, (p + 1) * WIDTH)
                normed[r : r + TILE, cols] = (centred[p] * rstd * gain[:, cols]).astype(BF16)
        here = pl.ds(pl.multiple_of(rows + CAP, CH), CH)
        x = normed[...]
        qk[0, here, :] = (jnp.dot(x, wq[0], preferred_element_type=F32) * QSCALE).astype(BF16)
        qk[1, here, :] = jnp.dot(x, wq[1], preferred_element_type=F32).astype(BF16)
        v = jnp.dot(x, wq[2], preferred_element_type=F32).astype(BF16)
        vv[0, here, 0:128] = v[:, 0:128]
        vv[1, here, 0:128] = v[:, 128:256]

    tail_qk = remote(qk.at[:, pl.ds(ROWS, CAP), :], qk.at[:, pl.ds(0, CAP), :], t_send.at[0], t_recv.at[0], to_after)
    tail_v = remote(
        vv.at[:, pl.ds(ROWS, CAP), pl.ds(0, 128)], vv.at[:, pl.ds(0, CAP), pl.ds(0, 128)],
        t_send.at[1], t_recv.at[1], to_after,
    )

    def arrive(i):
        gather_wait(0, i)
        gather_wait(1, i)
        gather_copy(2, i).start()
        gather_copy(3, i).start()

    def more(i):
        gather_copy(0, i).start()
        gather_copy(1, i).start()

    arrive(0)
    more(2)
    arrive(1)
    more(3)
    project(0)
    tail_qk.start()
    tail_v.start()
    arrive(2)
    project(1)
    arrive(3)

    lanes = lax.broadcasted_iota(jnp.int32, (1, 128), 1) < HS

    def attend(block, target, part=None, span=None):
        first, extent = bands[block] if span is None else span
        rows = slice(block * BLK, (block + 1) * BLK)
        span = slice(first, first + extent)

        def pair_step(pair, _):
            cols = pl.ds(pl.multiple_of(pair * 128, 128), 128)
            q = qk[0, rows, cols]
            for half in range(2):
                q_half = jnp.where(lanes if half == 0 else ~lanes, q, jnp.zeros_like(q))
                for k in range(0, extent, BLK):
                    score[half, :, k : k + BLK] = lax.dot_general(
                        q_half, qk[1, first + k : first + k + BLK, cols], (((1,), (1,)), ((), ())),
                        preferred_element_type=F32,
                    )
            results = []
            for half in range(2):
                for r in range(0, BLK, TILE):
                    tile = slice(r, r + TILE)
                    allowed = score[half, tile, 0:extent] + bias[block * BLK + r : block * BLK + r + TILE, span]
                    top = jnp.max(allowed, axis=1, keepdims=True)
                    if part == 0:
                        top_held[pair, half, tile, :] = jnp.broadcast_to(top, (TILE, 128))
                    elif part == 1:
                        old = top_held[pair, half, tile, :]
                        top = jnp.maximum(old[:, 0:1], top)
                        shrink[half, tile, :] = jnp.exp2(old - top)
                    prob[half, tile, 0:extent] = jnp.exp2(allowed - top).astype(BF16)
                results.append(jnp.dot(prob[half, :, 0:extent], vv[pair, span, :], preferred_element_type=F32))
            total = jnp.where(lanes, results[0][:, 0:128], results[1][:, 0:128])
            weight = jnp.where(lanes, results[0][:, 128:256], results[1][:, 128:256])
            if part == 0:
                held[pair, 0] = total
                held[pair, 1] = weight
            else:
                if part == 1:
                    scale = jnp.where(lanes, shrink[0], shrink[1])
                    total = total + scale * held[pair, 0]
                    weight = weight + scale * held[pair, 1]
                target[:, cols] = (total / weight).astype(BF16)
            return 0

        lax.fori_loop(0, 2, pair_step, 0)

    project(2)
    attend(3, att, 0, (512, 768))
    project(3)
    load_wo.wait()
    give_back = remote(attin, back, b_send, b_recv, to_before)

    half = BLK // 2
    low, high = pl.ds(0, half), pl.ds(half, half)

    def rs_copy(kind, b):
        src, dst, there = (
            (part.at[b, far, low, :], hop.at[b, 0], to_right),
            (part.at[b, far, high, :], hop.at[b, 1], to_left),
            (part.at[b, right, high, :], fin.at[b, 0, high, :], to_right),
            (part.at[b, left, low, :], fin.at[b, 1, low, :], to_left),
            (relay.at[b, 0], fin.at[b, 0, low, :], to_right),
            (relay.at[b, 1], fin.at[b, 1, high, :], to_left),
        )[kind]
        return remote(src, dst, rs_send.at[kind, b], rs_recv.at[kind, b], there)

    def pass_on(b):
        rs_copy(0, b).wait_recv()
        relay[b, 0] = (hop[b, 0].astype(F32) + part[b, right, low, :].astype(F32)).astype(BF16)
        rs_copy(4, b).start()
        rs_copy(1, b).wait_recv()
        relay[b, 1] = (hop[b, 1].astype(F32) + part[b, left, high, :].astype(F32)).astype(BF16)
        rs_copy(5, b).start()

    order = (2, 1, 0, 3)
    for step, b in enumerate(order):
        if step == 0:
            attend(3, att, 1, (256, 256))
        elif step == 1:
            admit()
            tail_qk.wait_recv()
            tail_v.wait_recv()
            attend(2, att)
        elif step == 2:
            attend(0, attin)
            give_back.start()
            attend(1, att)
        else:
            attend(4, att)
            give_back.wait_recv()
            moved = labcol[ALL - BLK : ALL, :] < 0.0
            for cols in (slice(0, 128), slice(128, 256)):
                att[:, cols] = jnp.where(moved, back[:, cols].astype(F32), att[:, cols].astype(F32)).astype(BF16)
        rows = att[...]
        for p in range(PARTS):
            part[b, p] = jnp.dot(
                rows, wo[:, p * WIDTH : (p + 1) * WIDTH], preferred_element_type=F32
            ).astype(BF16)
        for kind in range(4):
            rs_copy(kind, b).start()
        if step >= 1:
            pass_on(order[step - 1])

    def store_out(b):
        rows = pl.ds(b * BLK, BLK)
        return pltpu.make_async_copy(outv.at[rows, :], out_any.at[rows, :], out_sem.at[b])

    def finish(b):
        for kind in range(2, 6):
            rs_copy(kind, b).wait_recv()
        rows = slice(b * BLK, (b + 1) * BLK)
        outv[rows, :] = (
            xg[me, rows, :].astype(F32)
            + part[b, me].astype(F32)
            + fin[b, 0].astype(F32)
            + fin[b, 1].astype(F32)
        ).astype(BF16)
        store_out(b).start()

    finish(order[0])
    finish(order[1])
    pass_on(order[3])
    finish(order[2])
    finish(order[3])

    def drain(i, _):
        for kind in range(4):
            gather_copy(kind, i).wait_send()
        return 0

    lax.fori_loop(0, NCH, drain, 0)
    code.wait_send()
    tail_qk.wait_send()
    tail_v.wait_send()
    give_back.wait_send()
    for b in range(NBLK):
        for kind in range(6):
            rs_copy(kind, b).wait_send()
        store_out(b).wait()


def write_out(src, dst, sem):
    pieces = [
        pltpu.make_async_copy(src.at[pl.ds(b * BLK, BLK), :], dst.at[pl.ds(b * BLK, BLK), :], sem.at[b])
        for b in range(NBLK)
    ]
    for piece in pieces:
        piece.start()
    for piece in pieces:
        piece.wait()


def local(tokens, norm_gain, w_qkv, w_out, window_id, carry):
    there = pl.BlockSpec(memory_space=pltpu.HBM)
    dma = pltpu.SemaphoreType.DMA
    result = pl.pallas_call(
        kernel,
        out_shape=jax.ShapeDtypeStruct(tokens.shape, BF16),
        in_specs=[there] * 5 + [pl.BlockSpec(memory_space=pltpu.SMEM)],
        out_specs=pl.BlockSpec(memory_space=pl.ANY),
        scratch_shapes=[
            pltpu.VMEM((1, PARTS * WIDTH), F32),
            pltpu.VMEM((1, ROWS), jnp.int32),
            pltpu.VMEM((PARTS, ROWS, WIDTH), BF16),
            pltpu.VMEM((3, PARTS * WIDTH, WIDTH), BF16),
            pltpu.VMEM((WIDTH, PARTS * WIDTH), BF16),
            pltpu.VMEM((CH, PARTS * WIDTH), BF16),
            pltpu.VMEM((2, ALL, WIDTH), BF16),
            pltpu.VMEM((2, ALL, WIDTH), BF16),
            pltpu.VMEM((8, 128), F32),
            pltpu.VMEM((8, 128), F32),
            pltpu.VMEM((ALL, ALL), F32),
            pltpu.VMEM((ALL, 128), F32),
            pltpu.VMEM((CAP, WIDTH), BF16),
            pltpu.VMEM((BLK, WIDTH), BF16),
            pltpu.VMEM((CAP, WIDTH), BF16),
            pltpu.VMEM((NBLK, PARTS, BLK, WIDTH), BF16),
            pltpu.VMEM((NBLK, 2, BLK // 2, WIDTH), BF16),
            pltpu.VMEM((NBLK, 2, BLK // 2, WIDTH), BF16),
            pltpu.VMEM((NBLK, 2, BLK, WIDTH), BF16),
            pltpu.VMEM((2, BLK, ALL), F32),
            pltpu.VMEM((2, BLK, ALL), BF16),
            pltpu.VMEM((ROWS, WIDTH), BF16),
            pltpu.VMEM((2, 2, BLK, 128), F32),
            pltpu.VMEM((2, 2, BLK, 128), F32),
            pltpu.VMEM((2, BLK, 128), F32),
            dma,
            dma((4,)),
            dma((4, NCH)),
            dma((4, NCH)),
            dma,
            dma,
            dma((2,)),
            dma((2,)),
            dma,
            dma,
            dma((6, NBLK)),
            dma((6, NBLK)),
            dma((NBLK,)),
        ],
        compiler_params=pltpu.CompilerParams(
            collective_id=0, has_side_effects=True, vmem_limit_bytes=56 * 1024 * 1024
        ),
        cost_estimate=pl.CostEstimate(flops=4_000_000_000, bytes_accessed=4_000_000, transcendentals=5_000_000),
    )(tokens, norm_gain.reshape(1, PARTS * WIDTH), w_qkv, w_out, window_id, carry)
    anywhere = pl.BlockSpec(memory_space=pl.ANY)
    return pl.pallas_call(
        write_out,
        out_shape=jax.ShapeDtypeStruct(tokens.shape, BF16),
        in_specs=[anywhere],
        out_specs=anywhere,
        scratch_shapes=[dma((NBLK,))],
        compiler_params=pltpu.CompilerParams(vmem_limit_bytes=60 * 1024 * 1024),
    )(result)


def solution(mesh):
    return jax.shard_map(
        local,
        mesh=mesh,
        in_specs=(
            P("space", "head"),
            P(),
            P(None, None, "head"),
            P("head", None),
            P("space", None),
            P("space"),
        ),
        out_specs=P("space", "head"),
        check_vma=False,
    )
```

```python
import functools
import math

import jax
import jax.numpy as jnp
from jax import lax
from jax.experimental import pallas as pl
from jax.experimental.pallas import tpu as pltpu
from jax.sharding import PartitionSpec as P

MESH = pl.DeviceIdType.MESH
F32 = jnp.float32
BF16 = jnp.bfloat16

HS = 64
CAP = 256
ROWS = 1024
ALL = ROWS + CAP
WIDTH = 256
PARTS = 4
CH = 256
LANE = 128
NCH = ROWS // CH
BLK = 256
NBLK = ROWS // BLK
AHEAD = 2
TILE = 16
EPS = 1e-05
QSCALE = HS**-0.5 * math.log2(math.e)
NEG = -1e30


def chunk_at(i):
    return NCH - 1 - i


def kernel(
    tok_hbm, gain_hbm, wqkv_hbm, wout_hbm, wid_hbm, carry_ref, out_any,
    gain_ref, wid_ref, xg, wq, wo, normed, qq, kt, vv, lab, labin, bias, labcol, back, att, attin, part, hop, relay, fin,
    score, prob, outv, held, top_held, shrink,
    own_sem, wsem, ag_send, ag_recv, c_send, c_recv, t_send, t_recv, b_send, b_recv,
    rs_send, rs_recv, out_sem,
):
    me = lax.axis_index("head")
    spot = lax.axis_index("space")
    spots = lax.axis_size("space")
    right, left = lax.rem(me + 1, PARTS), lax.rem(me + PARTS - 1, PARTS)
    far = lax.rem(me + 2, PARTS)
    after, before = lax.rem(spot + 1, spots), lax.rem(spot + spots - 1, spots)
    to_right, to_left = {"head": right}, {"head": left}
    to_after, to_before = {"space": after}, {"space": before}

    own = pltpu.make_async_copy(tok_hbm, xg.at[me], own_sem)
    own.start()

    barrier = pltpu.get_barrier_semaphore()
    for there in (to_right, to_left, to_before):
        pl.semaphore_signal(barrier, inc=1, device_id=there, device_id_type=MESH)

    load_wid = pltpu.make_async_copy(wid_hbm, wid_ref, wsem.at[2])
    load_wid.start()
    load_gain = pltpu.make_async_copy(gain_hbm, gain_ref, wsem.at[3])
    load_gain.start()
    load_wq = pltpu.make_async_copy(wqkv_hbm, wq, wsem.at[0])
    load_wq.start()
    load_wo = pltpu.make_async_copy(wout_hbm, wo, wsem.at[1])
    load_wo.start()

    count = carry_ref[0]
    lab[...] = jnp.full(lab.shape, count, jnp.int32).astype(F32)
    own.wait()
    pl.semaphore_wait(barrier, 3)

    def remote(src, dst, send, recv, there):
        return pltpu.make_async_remote_copy(
            src_ref=src, dst_ref=dst, send_sem=send, recv_sem=recv, device_id=there, device_id_type=MESH
        )

    def gather_copy(kind, i):
        rows = chunk_at(i) * CH
        slot, start, size, there = (
            (me, rows, CH, to_right),
            (me, rows, CH, to_left),
            (left, rows, CH // 2, to_right),
            (right, rows + CH // 2, CH // 2, to_left),
        )[kind]
        view = xg.at[slot, pl.ds(pl.multiple_of(start, CH // 2), size), :]
        return remote(view, view, ag_send.at[kind, i], ag_recv.at[kind, i], there)

    def gather_wait(kind, i):
        rows = chunk_at(i) * CH
        slot, start, size = (
            (left, rows, CH),
            (right, rows, CH),
            (far, rows, CH // 2),
            (far, rows + CH // 2, CH // 2),
        )[kind]
        view = xg.at[slot, pl.ds(pl.multiple_of(start, CH // 2), size), :]
        remote(view, view, ag_send.at[kind, i], ag_recv.at[kind, i], to_right).wait_recv()

    for i in range(AHEAD):
        gather_copy(0, i).start()
        gather_copy(1, i).start()
    code = remote(lab, labin, c_send, c_recv, to_after)
    code.start()

    vv[:, :, LANE:] = jnp.ones((2, ALL, LANE), BF16)

    def columns_of(queries, first):
        for k in range(queries.shape[1] // LANE):
            piece = jnp.broadcast_to(queries[0:1, k * LANE : (k + 1) * LANE], (LANE, LANE))
            labcol[first + k * LANE : first + (k + 1) * LANE, :] = piece.T

    def allow(block, queries, first, start, stop):
        keys = jnp.where(queries < 0.0, -2.0, queries)
        rows = slice(block * BLK, (block + 1) * BLK)
        column = labcol[rows, :]
        for k in range(start, stop, LANE):
            bias[rows, k : k + LANE] = jnp.where(column == keys[0:1, k - first : k - first + LANE], 0.0, NEG)

    def labels_here():
        spread = jnp.broadcast_to(wid_ref[...].astype(F32), (8, ROWS))
        place = lax.broadcasted_iota(jnp.int32, (8, ROWS), 1)
        return jnp.where(place >= ROWS - count, -1.0, spread)

    bands = {0: (0, 768), 1: (0, 1024), 2: (0, 1280), 3: (256, 1024), 4: (512, 768)}
    load_wid.wait()
    mine = labels_here()
    columns_of(mine, CAP)
    for block in range(1, NBLK + 1):
        first, extent = bands[block]
        allow(block, mine, CAP, max(first, CAP), first + extent)

    def admit():
        code.wait_recv()
        place = lax.broadcasted_iota(jnp.int32, (8, CAP), 1).astype(F32)
        theirs = jnp.where(place >= CAP - labin[0:1, 0:1], 0.0, -1.0)
        columns_of(theirs, 0)
        for block in range(3):
            allow(block, theirs, 0, 0, CAP)
        allow(0, labels_here(), CAP, CAP, 768)

    load_gain.wait()
    load_wq.wait()
    gain = gain_ref[...]

    def project(i):
        gather_wait(2, i)
        gather_wait(3, i)
        rows = chunk_at(i) * CH
        for r in range(0, CH, TILE):
            slices = [
                xg[p, rows + r : rows + r + TILE, :].astype(F32) for p in range(PARTS)
            ]
            mean = jnp.sum(sum(slices), axis=1, keepdims=True) * (1.0 / (PARTS * WIDTH))
            centred = [x - mean for x in slices]
            var = jnp.sum(sum(x * x for x in centred), axis=1, keepdims=True) * (1.0 / (PARTS * WIDTH))
            rstd = lax.rsqrt(var + EPS)
            for p in range(PARTS):
                cols = slice(p * WIDTH, (p + 1) * WIDTH)
                normed[r : r + TILE, cols] = (centred[p] * rstd * gain[:, cols]).astype(BF16)
        here = pl.ds(rows + CAP, CH)
        x = normed[...]
        qq[here, :] = (jnp.dot(x, wq[0], preferred_element_type=F32) * QSCALE).astype(BF16)
        kt[:, here] = jnp.dot(x, wq[1], preferred_element_type=F32).T.astype(BF16)
        v = jnp.dot(x, wq[2], preferred_element_type=F32).astype(BF16)
        vv[0, here, 0:128] = v[:, 0:128]
        vv[1, here, 0:128] = v[:, 128:256]

    tail_q = remote(qq.at[pl.ds(ROWS, CAP), :], qq.at[pl.ds(0, CAP), :], t_send.at[0], t_recv.at[0], to_after)
    tail_k = remote(kt.at[:, pl.ds(ROWS, CAP)], kt.at[:, pl.ds(0, CAP)], t_send.at[2], t_recv.at[2], to_after)
    tail_v = remote(
        vv.at[:, pl.ds(ROWS, CAP), pl.ds(0, 128)], vv.at[:, pl.ds(0, CAP), pl.ds(0, 128)],
        t_send.at[1], t_recv.at[1], to_after,
    )

    def arrive(i):
        gather_wait(0, i)
        gather_wait(1, i)
        gather_copy(2, i).start()
        gather_copy(3, i).start()

    def more(i):
        gather_copy(0, i).start()
        gather_copy(1, i).start()

    arrive(0)
    more(2)
    arrive(1)
    more(3)
    project(0)
    tail_q.start()
    tail_k.start()
    tail_v.start()
    arrive(2)
    project(1)
    arrive(3)

    lanes = lax.broadcasted_iota(jnp.int32, (1, 128), 1) < HS

    def attend(block, target, part=None, span=None):
        first, extent = bands[block] if span is None else span
        rows = slice(block * BLK, (block + 1) * BLK)
        span = slice(first, first + extent)

        def pair_step(pair, _):
            cols = pl.ds(pl.multiple_of(pair * 128, 128), 128)
            q = qq[rows, cols]
            for half in range(2):
                q_half = jnp.where(lanes if half == 0 else ~lanes, q, jnp.zeros_like(q))
                for k in range(0, extent, BLK):
                    score[half, :, k : k + BLK] = jnp.dot(
                        q_half, kt[cols, first + k : first + k + BLK], preferred_element_type=F32
                    )
            results = []
            for half in range(2):
                for r in range(0, BLK, TILE):
                    tile = slice(r, r + TILE)
                    allowed = score[half, tile, 0:extent] + bias[block * BLK + r : block * BLK + r + TILE, span]
                    top = jnp.max(allowed, axis=1, keepdims=True)
                    if part == 0:
                        top_held[pair, half, tile, :] = jnp.broadcast_to(top, (TILE, 128))
                    elif part == 1:
                        old = top_held[pair, half, tile, :]
                        top = jnp.maximum(old[:, 0:1], top)
                        shrink[half, tile, :] = jnp.exp2(old - top)
                    prob[half, tile, 0:extent] = jnp.exp2(allowed - top).astype(BF16)
                results.append(jnp.dot(prob[half, :, 0:extent], vv[pair, span, :], preferred_element_type=F32))
            total = jnp.where(lanes, results[0][:, 0:128], results[1][:, 0:128])
            weight = jnp.where(lanes, results[0][:, 128:256], results[1][:, 128:256])
            if part == 0:
                held[pair, 0] = total
                held[pair, 1] = weight
            else:
                if part == 1:
                    scale = jnp.where(lanes, shrink[0], shrink[1])
                    total = total + scale * held[pair, 0]
                    weight = weight + scale * held[pair, 1]
                target[:, cols] = (total / weight).astype(BF16)
            return 0

        lax.fori_loop(0, 2, pair_step, 0)

    project(2)
    attend(3, att, 0, (512, 768))
    project(3)
    load_wo.wait()
    give_back = remote(attin, back, b_send, b_recv, to_before)

    half = BLK // 2
    low, high = pl.ds(0, half), pl.ds(half, half)

    def rs_copy(kind, b):
        src, dst, there = (
            (part.at[b, far, low, :], hop.at[b, 0], to_right),
            (part.at[b, far, high, :], hop.at[b, 1], to_left),
            (part.at[b, right, high, :], fin.at[b, 0, high, :], to_right),
            (part.at[b, left, low, :], fin.at[b, 1, low, :], to_left),
            (relay.at[b, 0], fin.at[b, 0, low, :], to_right),
            (relay.at[b, 1], fin.at[b, 1, high, :], to_left),
        )[kind]
        return remote(src, dst, rs_send.at[kind, b], rs_recv.at[kind, b], there)

    def pass_on(b):
        rs_copy(0, b).wait_recv()
        relay[b, 0] = (hop[b, 0].astype(F32) + part[b, right, low, :].astype(F32)).astype(BF16)
        rs_copy(4, b).start()
        rs_copy(1, b).wait_recv()
        relay[b, 1] = (hop[b, 1].astype(F32) + part[b, left, high, :].astype(F32)).astype(BF16)
        rs_copy(5, b).start()

    order = (2, 1, 0, 3)
    for step, b in enumerate(order):
        if step == 0:
            attend(3, att, 1, (256, 256))
        elif step == 1:
            admit()
            tail_q.wait_recv()
            tail_k.wait_recv()
            tail_v.wait_recv()
            attend(2, att)
        elif step == 2:
            attend(0, attin)
            give_back.start()
            pass_on(order[1])
            attend(1, att)
        else:
            attend(4, att)
            pass_on(order[2])
            give_back.wait_recv()
            moved = labcol[ALL - BLK : ALL, :] < 0.0
            for cols in (slice(0, 128), slice(128, 256)):
                att[:, cols] = jnp.where(moved, back[:, cols].astype(F32), att[:, cols].astype(F32)).astype(BF16)
        rows = att[...]
        for p in range(PARTS):
            part[b, p] = jnp.dot(
                rows, wo[:, p * WIDTH : (p + 1) * WIDTH], preferred_element_type=F32
            ).astype(BF16)
        for kind in range(4):
            rs_copy(kind, b).start()
        if step == 1:
            pass_on(order[0])

    def store_out(b):
        rows = pl.ds(b * BLK, BLK)
        return pltpu.make_async_copy(outv.at[rows, :], out_any.at[rows, :], out_sem.at[b])

    def finish(b):
        for kind in range(2, 6):
            rs_copy(kind, b).wait_recv()
        rows = slice(b * BLK, (b + 1) * BLK)
        outv[rows, :] = (
            xg[me, rows, :].astype(F32)
            + part[b, me].astype(F32)
            + fin[b, 0].astype(F32)
            + fin[b, 1].astype(F32)
        ).astype(BF16)
        store_out(b).start()

    finish(order[0])
    finish(order[1])
    pass_on(order[3])
    finish(order[2])
    finish(order[3])

    def drain(i, _):
        for kind in range(4):
            gather_copy(kind, i).wait_send()
        return 0

    lax.fori_loop(0, NCH, drain, 0)
    code.wait_send()
    tail_q.wait_send()
    tail_k.wait_send()
    tail_v.wait_send()
    give_back.wait_send()
    for b in range(NBLK):
        for kind in range(6):
            rs_copy(kind, b).wait_send()
        store_out(b).wait()


def local(tokens, norm_gain, w_qkv, w_out, window_id, carry):
    there = pl.BlockSpec(memory_space=pltpu.HBM)
    dma = pltpu.SemaphoreType.DMA
    return pl.pallas_call(
        kernel,
        out_shape=jax.ShapeDtypeStruct(tokens.shape, BF16),
        in_specs=[there] * 5 + [pl.BlockSpec(memory_space=pltpu.SMEM)],
        out_specs=pl.BlockSpec(memory_space=pl.ANY),
        scratch_shapes=[
            pltpu.VMEM((1, PARTS * WIDTH), F32),
            pltpu.VMEM((1, ROWS), jnp.int32),
            pltpu.VMEM((PARTS, ROWS, WIDTH), BF16),
            pltpu.VMEM((3, PARTS * WIDTH, WIDTH), BF16),
            pltpu.VMEM((WIDTH, PARTS * WIDTH), BF16),
            pltpu.VMEM((CH, PARTS * WIDTH), BF16),
            pltpu.VMEM((ALL, WIDTH), BF16),
            pltpu.VMEM((WIDTH, ALL), BF16),
            pltpu.VMEM((2, ALL, WIDTH), BF16),
            pltpu.VMEM((8, 128), F32),
            pltpu.VMEM((8, 128), F32),
            pltpu.VMEM((ALL, ALL), F32),
            pltpu.VMEM((ALL, 128), F32),
            pltpu.VMEM((CAP, WIDTH), BF16),
            pltpu.VMEM((BLK, WIDTH), BF16),
            pltpu.VMEM((CAP, WIDTH), BF16),
            pltpu.VMEM((NBLK, PARTS, BLK, WIDTH), BF16),
            pltpu.VMEM((NBLK, 2, BLK // 2, WIDTH), BF16),
            pltpu.VMEM((NBLK, 2, BLK // 2, WIDTH), BF16),
            pltpu.VMEM((NBLK, 2, BLK, WIDTH), BF16),
            pltpu.VMEM((2, BLK, ALL), F32),
            pltpu.VMEM((2, BLK, ALL), BF16),
            pltpu.VMEM((ROWS, WIDTH), BF16),
            pltpu.VMEM((2, 2, BLK, 128), F32),
            pltpu.VMEM((2, 2, BLK, 128), F32),
            pltpu.VMEM((2, BLK, 128), F32),
            dma,
            dma((4,)),
            dma((4, NCH)),
            dma((4, NCH)),
            dma,
            dma,
            dma((3,)),
            dma((3,)),
            dma,
            dma,
            dma((6, NBLK)),
            dma((6, NBLK)),
            dma((NBLK,)),
        ],
        compiler_params=pltpu.CompilerParams(
            collective_id=0, has_side_effects=True, vmem_limit_bytes=56 * 1024 * 1024
        ),
        cost_estimate=pl.CostEstimate(flops=4_000_000_000, bytes_accessed=4_000_000, transcendentals=5_000_000),
    )(tokens, norm_gain.reshape(1, PARTS * WIDTH), w_qkv, w_out, window_id, carry)


def solution(mesh):
    return jax.shard_map(
        local,
        mesh=mesh,
        in_specs=(
            P("space", "head"),
            P(),
            P(None, None, "head"),
            P("head", None),
            P("space", None),
            P("space"),
        ),
        out_specs=P("space", "head"),
        check_vma=False,
    )
```

```python
import functools
import math

import jax
import jax.numpy as jnp
from jax import lax
from jax.experimental import pallas as pl
from jax.experimental.pallas import tpu as pltpu
from jax.sharding import PartitionSpec as P

MESH = pl.DeviceIdType.MESH
F32 = jnp.float32
BF16 = jnp.bfloat16

HS = 64
CAP = 256
ROWS = 1024
ALL = ROWS + CAP
WIDTH = 256
PARTS = 4
CH = 256
LANE = 128
NCH = ROWS // CH
BLK = 256
NBLK = ROWS // BLK
AHEAD = 2
TILE = 16
EPS = 1e-05
QSCALE = HS**-0.5 * math.log2(math.e)
NEG = -1e30


def chunk_at(i):
    return NCH - 1 - i


def kernel(
    tok_hbm, gain_hbm, wqkv_hbm, wout_hbm, wid_hbm, carry_ref, out_any,
    gain_ref, wid_ref, xg, wq, wo, normed, qk, vv, lab, labin, bias, labcol, back, att, attin, part, hop, relay, fin,
    score, prob, outv, held, top_held, shrink,
    own_sem, wsem, ag_send, ag_recv, c_send, c_recv, t_send, t_recv, b_send, b_recv,
    rs_send, rs_recv, out_sem,
):
    me = lax.axis_index("head")
    spot = lax.axis_index("space")
    spots = lax.axis_size("space")
    right, left = lax.rem(me + 1, PARTS), lax.rem(me + PARTS - 1, PARTS)
    far = lax.rem(me + 2, PARTS)
    after, before = lax.rem(spot + 1, spots), lax.rem(spot + spots - 1, spots)
    to_right, to_left = {"head": right}, {"head": left}
    to_after, to_before = {"space": after}, {"space": before}

    own = pltpu.make_async_copy(tok_hbm, xg.at[me], own_sem)
    own.start()

    barrier = pltpu.get_barrier_semaphore()
    for there in (to_right, to_left, to_before):
        pl.semaphore_signal(barrier, inc=1, device_id=there, device_id_type=MESH)

    load_wid = pltpu.make_async_copy(wid_hbm, wid_ref, wsem.at[2])
    load_wid.start()
    load_gain = pltpu.make_async_copy(gain_hbm, gain_ref, wsem.at[3])
    load_gain.start()
    load_wq = pltpu.make_async_copy(wqkv_hbm, wq, wsem.at[0])
    load_wq.start()
    load_wo = pltpu.make_async_copy(wout_hbm, wo, wsem.at[1])
    load_wo.start()

    count = carry_ref[0]
    lab[...] = jnp.full(lab.shape, count, jnp.int32).astype(F32)
    own.wait()
    pl.semaphore_wait(barrier, 3)

    def remote(src, dst, send, recv, there):
        return pltpu.make_async_remote_copy(
            src_ref=src, dst_ref=dst, send_sem=send, recv_sem=recv, device_id=there, device_id_type=MESH
        )

    def gather_copy(kind, i):
        rows = chunk_at(i) * CH
        slot, start, size, there = (
            (me, rows, CH, to_right),
            (me, rows, CH, to_left),
            (left, rows, CH // 2, to_right),
            (right, rows + CH // 2, CH // 2, to_left),
        )[kind]
        view = xg.at[slot, pl.ds(pl.multiple_of(start, CH // 2), size), :]
        return remote(view, view, ag_send.at[kind, i], ag_recv.at[kind, i], there)

    def gather_wait(kind, i):
        rows = chunk_at(i) * CH
        slot, start, size = (
            (left, rows, CH),
            (right, rows, CH),
            (far, rows, CH // 2),
            (far, rows + CH // 2, CH // 2),
        )[kind]
        view = xg.at[slot, pl.ds(pl.multiple_of(start, CH // 2), size), :]
        remote(view, view, ag_send.at[kind, i], ag_recv.at[kind, i], to_right).wait_recv()

    for i in range(AHEAD):
        gather_copy(0, i).start()
        gather_copy(1, i).start()
    code = remote(lab, labin, c_send, c_recv, to_after)
    code.start()

    vv[:, :, LANE:] = jnp.ones((2, ALL, LANE), BF16)

    def columns_of(queries, first):
        for k in range(queries.shape[1] // LANE):
            piece = jnp.broadcast_to(queries[0:1, k * LANE : (k + 1) * LANE], (LANE, LANE))
            labcol[first + k * LANE : first + (k + 1) * LANE, :] = piece.T

    def allow(block, queries, first, start, stop):
        keys = jnp.where(queries < 0.0, -2.0, queries)
        rows = slice(block * BLK, (block + 1) * BLK)
        column = labcol[rows, :]
        for k in range(start, stop, LANE):
            bias[rows, k : k + LANE] = jnp.where(column == keys[0:1, k - first : k - first + LANE], 0.0, NEG)

    def labels_here():
        spread = jnp.broadcast_to(wid_ref[...].astype(F32), (8, ROWS))
        place = lax.broadcasted_iota(jnp.int32, (8, ROWS), 1)
        return jnp.where(place >= ROWS - count, -1.0, spread)

    bands = {0: (0, 768), 1: (0, 1024), 2: (0, 1280), 3: (256, 1024), 4: (512, 768)}
    load_wid.wait()
    mine = labels_here()
    columns_of(mine, CAP)
    for block in range(1, NBLK + 1):
        first, extent = bands[block]
        allow(block, mine, CAP, max(first, CAP), first + extent)

    def admit():
        code.wait_recv()
        place = lax.broadcasted_iota(jnp.int32, (8, CAP), 1).astype(F32)
        theirs = jnp.where(place >= CAP - labin[0:1, 0:1], 0.0, -1.0)
        columns_of(theirs, 0)
        for block in range(3):
            allow(block, theirs, 0, 0, CAP)
        allow(0, labels_here(), CAP, CAP, 768)

    load_gain.wait()
    load_wq.wait()
    gain = gain_ref[...]

    def project(i):
        gather_wait(2, i)
        gather_wait(3, i)
        rows = pl.multiple_of(chunk_at(i) * CH, CH)
        for r in range(0, CH, TILE):
            slices = [
                xg[p, pl.ds(pl.multiple_of(rows + r, TILE), TILE), :].astype(F32) for p in range(PARTS)
            ]
            mean = jnp.sum(sum(slices), axis=1, keepdims=True) * (1.0 / (PARTS * WIDTH))
            centred = [x - mean for x in slices]
            var = jnp.sum(sum(x * x for x in centred), axis=1, keepdims=True) * (1.0 / (PARTS * WIDTH))
            rstd = lax.rsqrt(var + EPS)
            for p in range(PARTS):
                cols = slice(p * WIDTH, (p + 1) * WIDTH)
                normed[r : r + TILE, cols] = (centred[p] * rstd * gain[:, cols]).astype(BF16)
        here = pl.ds(pl.multiple_of(rows + CAP, CH), CH)
        x = normed[...]
        qk[0, here, :] = (jnp.dot(x, wq[0], preferred_element_type=F32) * QSCALE).astype(BF16)
        qk[1, here, :] = jnp.dot(x, wq[1], preferred_element_type=F32).astype(BF16)
        v = jnp.dot(x, wq[2], preferred_element_type=F32).astype(BF16)
        vv[0, here, 0:128] = v[:, 0:128]
        vv[1, here, 0:128] = v[:, 128:256]

    tail_qk = remote(qk.at[:, pl.ds(ROWS, CAP), :], qk.at[:, pl.ds(0, CAP), :], t_send.at[0], t_recv.at[0], to_after)
    tail_v = remote(
        vv.at[:, pl.ds(ROWS, CAP), pl.ds(0, 128)], vv.at[:, pl.ds(0, CAP), pl.ds(0, 128)],
        t_send.at[1], t_recv.at[1], to_after,
    )

    def arrive(i):
        gather_wait(0, i)
        gather_wait(1, i)
        gather_copy(2, i).start()
        gather_copy(3, i).start()

    def more(i):
        gather_copy(0, i).start()
        gather_copy(1, i).start()

    arrive(0)
    more(2)
    arrive(1)
    more(3)
    project(0)
    tail_qk.start()
    tail_v.start()
    arrive(2)
    project(1)
    arrive(3)

    lanes = lax.broadcasted_iota(jnp.int32, (1, 128), 1) < HS

    def attend(block, target, part=None, span=None):
        first, extent = bands[block] if span is None else span
        rows = slice(block * BLK, (block + 1) * BLK)
        span = slice(first, first + extent)

        def pair_step(pair, _):
            cols = pl.ds(pl.multiple_of(pair * 128, 128), 128)
            q = qk[0, rows, cols]
            for half in range(2):
                q_half = jnp.where(lanes if half == 0 else ~lanes, q, jnp.zeros_like(q))
                for k in range(0, extent, BLK):
                    score[half, :, k : k + BLK] = lax.dot_general(
                        q_half, qk[1, first + k : first + k + BLK, cols], (((1,), (1,)), ((), ())),
                        preferred_element_type=F32,
                    )
            results = []
            for half in range(2):
                for r in range(0, BLK, TILE):
                    tile = slice(r, r + TILE)
                    allowed = score[half, tile, 0:extent] + bias[block * BLK + r : block * BLK + r + TILE, span]
                    top = jnp.max(allowed, axis=1, keepdims=True)
                    if part == 0:
                        top_held[pair, half, tile, :] = jnp.broadcast_to(top, (TILE, 128))
                    elif part == 1:
                        old = top_held[pair, half, tile, :]
                        top = jnp.maximum(old[:, 0:1], top)
                        shrink[half, tile, :] = jnp.exp2(old - top)
                    prob[half, tile, 0:extent] = jnp.exp2(allowed - top).astype(BF16)
                results.append(jnp.dot(prob[half, :, 0:extent], vv[pair, span, :], preferred_element_type=F32))
            total = jnp.where(lanes, results[0][:, 0:128], results[1][:, 0:128])
            weight = jnp.where(lanes, results[0][:, 128:256], results[1][:, 128:256])
            if part == 0:
                held[pair, 0] = total
                held[pair, 1] = weight
            else:
                if part == 1:
                    scale = jnp.where(lanes, shrink[0], shrink[1])
                    total = total + scale * held[pair, 0]
                    weight = weight + scale * held[pair, 1]
                target[:, cols] = (total / weight).astype(BF16)
            return 0

        lax.fori_loop(0, 2, pair_step, 0)

    project(2)
    attend(3, att, 0, (512, 768))
    project(3)
    load_wo.wait()
    give_back = remote(attin, back, b_send, b_recv, to_before)

    half = BLK // 2
    low, high = pl.ds(0, half), pl.ds(half, half)

    def rs_copy(kind, b):
        src, dst, there = (
            (part.at[b, far, low, :], hop.at[b, 0], to_right),
            (part.at[b, far, high, :], hop.at[b, 1], to_left),
            (part.at[b, right, high, :], fin.at[b, 0, high, :], to_right),
            (part.at[b, left, low, :], fin.at[b, 1, low, :], to_left),
            (relay.at[b, 0], fin.at[b, 0, low, :], to_right),
            (relay.at[b, 1], fin.at[b, 1, high, :], to_left),
        )[kind]
        return remote(src, dst, rs_send.at[kind, b], rs_recv.at[kind, b], there)

    def pass_on(b):
        rs_copy(0, b).wait_recv()
        relay[b, 0] = (hop[b, 0].astype(F32) + part[b, right, low, :].astype(F32)).astype(BF16)
        rs_copy(4, b).start()
        rs_copy(1, b).wait_recv()
        relay[b, 1] = (hop[b, 1].astype(F32) + part[b, left, high, :].astype(F32)).astype(BF16)
        rs_copy(5, b).start()

    order = (2, 1, 0, 3)
    for step, b in enumerate(order):
        if step == 0:
            attend(3, att, 1, (256, 256))
        elif step == 1:
            admit()
            tail_qk.wait_recv()
            tail_v.wait_recv()
            attend(2, att)
        elif step == 2:
            attend(0, attin)
            give_back.start()
            attend(1, att)
        else:
            attend(4, att)
            give_back.wait_recv()
            moved = labcol[ALL - BLK : ALL, :] < 0.0
            for cols in (slice(0, 128), slice(128, 256)):
                att[:, cols] = jnp.where(moved, back[:, cols].astype(F32), att[:, cols].astype(F32)).astype(BF16)
        rows = att[...]
        for p in range(PARTS):
            part[b, p] = jnp.dot(
                rows, wo[:, p * WIDTH : (p + 1) * WIDTH], preferred_element_type=F32
            ).astype(BF16)
        for kind in range(4):
            rs_copy(kind, b).start()
        if step >= 1:
            pass_on(order[step - 1])

    def store_out(b):
        rows = pl.ds(b * BLK, BLK)
        return pltpu.make_async_copy(outv.at[rows, :], out_any.at[rows, :], out_sem.at[b])

    def finish(b):
        for kind in range(2, 6):
            rs_copy(kind, b).wait_recv()
        rows = slice(b * BLK, (b + 1) * BLK)
        outv[rows, :] = (
            xg[me, rows, :].astype(F32)
            + part[b, me].astype(F32)
            + fin[b, 0].astype(F32)
            + fin[b, 1].astype(F32)
        ).astype(BF16)
        store_out(b).start()

    finish(order[0])
    pass_on(order[3])
    finish(order[1])
    finish(order[2])
    finish(order[3])

    def drain(i, _):
        for kind in range(4):
            gather_copy(kind, i).wait_send()
        return 0

    lax.fori_loop(0, NCH, drain, 0)
    code.wait_send()
    tail_qk.wait_send()
    tail_v.wait_send()
    give_back.wait_send()
    for b in range(NBLK):
        for kind in range(6):
            rs_copy(kind, b).wait_send()
        store_out(b).wait()


def local(tokens, norm_gain, w_qkv, w_out, window_id, carry):
    there = pl.BlockSpec(memory_space=pltpu.HBM)
    dma = pltpu.SemaphoreType.DMA
    return pl.pallas_call(
        kernel,
        out_shape=jax.ShapeDtypeStruct(tokens.shape, BF16),
        in_specs=[there] * 5 + [pl.BlockSpec(memory_space=pltpu.SMEM)],
        out_specs=pl.BlockSpec(memory_space=pl.ANY),
        scratch_shapes=[
            pltpu.VMEM((1, PARTS * WIDTH), F32),
            pltpu.VMEM((1, ROWS), jnp.int32),
            pltpu.VMEM((PARTS, ROWS, WIDTH), BF16),
            pltpu.VMEM((3, PARTS * WIDTH, WIDTH), BF16),
            pltpu.VMEM((WIDTH, PARTS * WIDTH), BF16),
            pltpu.VMEM((CH, PARTS * WIDTH), BF16),
            pltpu.VMEM((2, ALL, WIDTH), BF16),
            pltpu.VMEM((2, ALL, WIDTH), BF16),
            pltpu.VMEM((8, 128), F32),
            pltpu.VMEM((8, 128), F32),
            pltpu.VMEM((ALL, ALL), F32),
            pltpu.VMEM((ALL, 128), F32),
            pltpu.VMEM((CAP, WIDTH), BF16),
            pltpu.VMEM((BLK, WIDTH), BF16),
            pltpu.VMEM((CAP, WIDTH), BF16),
            pltpu.VMEM((NBLK, PARTS, BLK, WIDTH), BF16),
            pltpu.VMEM((NBLK, 2, BLK // 2, WIDTH), BF16),
            pltpu.VMEM((NBLK, 2, BLK // 2, WIDTH), BF16),
            pltpu.VMEM((NBLK, 2, BLK, WIDTH), BF16),
            pltpu.VMEM((2, BLK, ALL), F32),
            pltpu.VMEM((2, BLK, ALL), BF16),
            pltpu.VMEM((ROWS, WIDTH), BF16),
            pltpu.VMEM((2, 2, BLK, 128), F32),
            pltpu.VMEM((2, 2, BLK, 128), F32),
            pltpu.VMEM((2, BLK, 128), F32),
            dma,
            dma((4,)),
            dma((4, NCH)),
            dma((4, NCH)),
            dma,
            dma,
            dma((2,)),
            dma((2,)),
            dma,
            dma,
            dma((6, NBLK)),
            dma((6, NBLK)),
            dma((NBLK,)),
        ],
        compiler_params=pltpu.CompilerParams(
            collective_id=0, has_side_effects=True, vmem_limit_bytes=56 * 1024 * 1024
        ),
        cost_estimate=pl.CostEstimate(flops=4_000_000_000, bytes_accessed=4_000_000, transcendentals=5_000_000),
    )(tokens, norm_gain.reshape(1, PARTS * WIDTH), w_qkv, w_out, window_id, carry)


def solution(mesh):
    return jax.shard_map(
        local,
        mesh=mesh,
        in_specs=(
            P("space", "head"),
            P(),
            P(None, None, "head"),
            P("head", None),
            P("space", None),
            P("space"),
        ),
        out_specs=P("space", "head"),
        check_vma=False,
    )
```

```python
import functools
import math

import jax
import jax.numpy as jnp
from jax import lax
from jax.experimental import pallas as pl
from jax.experimental.pallas import tpu as pltpu
from jax.sharding import PartitionSpec as P

MESH = pl.DeviceIdType.MESH
F32 = jnp.float32
BF16 = jnp.bfloat16

HS = 64
CAP = 256
ROWS = 1024
ALL = ROWS + CAP
WIDTH = 256
PARTS = 4
CH = 256
LANE = 128
NCH = ROWS // CH
BLK = 256
NBLK = ROWS // BLK
AHEAD = 2
TILE = 16
EPS = 1e-05
QSCALE = HS**-0.5 * math.log2(math.e)
NEG = -1e30


def chunk_at(i):
    return NCH - 1 - i


def kernel(
    tok_hbm, gain_hbm, wqkv_hbm, wout_hbm, wid_hbm, carry_ref, out_any,
    gain_ref, wid_ref, xg, wq, wo, normed, qk, vv, lab, labin, bias, labcol, back, att, attin, part, hop, relay, fin,
    score, prob, outv, held, top_held, shrink,
    own_sem, wsem, ag_send, ag_recv, c_send, c_recv, t_send, t_recv, b_send, b_recv,
    rs_send, rs_recv, out_sem,
):
    me = lax.axis_index("head")
    spot = lax.axis_index("space")
    spots = lax.axis_size("space")
    right, left = lax.rem(me + 1, PARTS), lax.rem(me + PARTS - 1, PARTS)
    far = lax.rem(me + 2, PARTS)
    after, before = lax.rem(spot + 1, spots), lax.rem(spot + spots - 1, spots)
    to_right, to_left = {"head": right}, {"head": left}
    to_after, to_before = {"space": after}, {"space": before}

    own = pltpu.make_async_copy(tok_hbm, xg.at[me], own_sem)
    own.start()

    barrier = pltpu.get_barrier_semaphore()
    for there in (to_right, to_left, to_before):
        pl.semaphore_signal(barrier, inc=1, device_id=there, device_id_type=MESH)

    load_wid = pltpu.make_async_copy(wid_hbm, wid_ref, wsem.at[2])
    load_wid.start()
    load_gain = pltpu.make_async_copy(gain_hbm, gain_ref, wsem.at[3])
    load_gain.start()
    load_wq = pltpu.make_async_copy(wqkv_hbm, wq, wsem.at[0])
    load_wq.start()
    load_wo = pltpu.make_async_copy(wout_hbm, wo, wsem.at[1])
    load_wo.start()

    count = carry_ref[0]
    lab[...] = jnp.full(lab.shape, count, jnp.int32).astype(F32)
    own.wait()
    pl.semaphore_wait(barrier, 3)

    def remote(src, dst, send, recv, there):
        return pltpu.make_async_remote_copy(
            src_ref=src, dst_ref=dst, send_sem=send, recv_sem=recv, device_id=there, device_id_type=MESH
        )

    def gather_copy(kind, i):
        rows = chunk_at(i) * CH
        slot, start, size, there = (
            (me, rows, CH, to_right),
            (me, rows, CH, to_left),
            (left, rows, CH // 2, to_right),
            (right, rows + CH // 2, CH // 2, to_left),
        )[kind]
        view = xg.at[slot, pl.ds(pl.multiple_of(start, CH // 2), size), :]
        return remote(view, view, ag_send.at[kind, i], ag_recv.at[kind, i], there)

    def gather_wait(kind, i):
        rows = chunk_at(i) * CH
        slot, start, size = (
            (left, rows, CH),
            (right, rows, CH),
            (far, rows, CH // 2),
            (far, rows + CH // 2, CH // 2),
        )[kind]
        view = xg.at[slot, pl.ds(pl.multiple_of(start, CH // 2), size), :]
        remote(view, view, ag_send.at[kind, i], ag_recv.at[kind, i], to_right).wait_recv()

    for i in range(AHEAD):
        gather_copy(0, i).start()
        gather_copy(1, i).start()
    code = remote(lab, labin, c_send, c_recv, to_after)
    code.start()

    vv[:, :, LANE:] = jnp.ones((2, ALL, LANE), BF16)

    def columns_of(queries, first):
        for k in range(queries.shape[1] // LANE):
            piece = jnp.broadcast_to(queries[0:1, k * LANE : (k + 1) * LANE], (LANE, LANE))
            labcol[first + k * LANE : first + (k + 1) * LANE, :] = piece.T

    def allow(block, queries, first, start, stop):
        keys = jnp.where(queries < 0.0, -2.0, queries)
        rows = slice(block * BLK, (block + 1) * BLK)
        column = labcol[rows, :]
        for k in range(start, stop, LANE):
            bias[rows, k : k + LANE] = jnp.where(column == keys[0:1, k - first : k - first + LANE], 0.0, NEG)

    def labels_here():
        spread = jnp.broadcast_to(wid_ref[...].astype(F32), (8, ROWS))
        place = lax.broadcasted_iota(jnp.int32, (8, ROWS), 1)
        return jnp.where(place >= ROWS - count, -1.0, spread)

    bands = {0: (0, 768), 1: (0, 1024), 2: (0, 1280), 3: (256, 1024), 4: (512, 768)}
    load_wid.wait()
    mine = labels_here()
    columns_of(mine, CAP)
    for block in range(1, NBLK + 1):
        first, extent = bands[block]
        allow(block, mine, CAP, max(first, CAP), first + extent)

    def admit():
        code.wait_recv()
        place = lax.broadcasted_iota(jnp.int32, (8, CAP), 1).astype(F32)
        theirs = jnp.where(place >= CAP - labin[0:1, 0:1], 0.0, -1.0)
        columns_of(theirs, 0)
        for block in range(3):
            allow(block, theirs, 0, 0, CAP)
        allow(0, labels_here(), CAP, CAP, 768)

    load_gain.wait()
    load_wq.wait()
    gain = gain_ref[...]

    def project(i):
        gather_wait(2, i)
        gather_wait(3, i)
        rows = pl.multiple_of(chunk_at(i) * CH, CH)
        for r in range(0, CH, TILE):
            slices = [
                xg[p, pl.ds(pl.multiple_of(rows + r, TILE), TILE), :].astype(F32) for p in range(PARTS)
            ]
            mean = jnp.sum(sum(slices), axis=1, keepdims=True) * (1.0 / (PARTS * WIDTH))
            centred = [x - mean for x in slices]
            var = jnp.sum(sum(x * x for x in centred), axis=1, keepdims=True) * (1.0 / (PARTS * WIDTH))
            rstd = lax.rsqrt(var + EPS)
            for p in range(PARTS):
                cols = slice(p * WIDTH, (p + 1) * WIDTH)
                normed[r : r + TILE, cols] = (centred[p] * rstd * gain[:, cols]).astype(BF16)
        here = pl.ds(pl.multiple_of(rows + CAP, CH), CH)
        x = normed[...]
        qk[0, here, :] = (jnp.dot(x, wq[0], preferred_element_type=F32) * QSCALE).astype(BF16)
        qk[1, here, :] = jnp.dot(x, wq[1], preferred_element_type=F32).astype(BF16)
        v = jnp.dot(x, wq[2], preferred_element_type=F32).astype(BF16)
        vv[0, here, 0:128] = v[:, 0:128]
        vv[1, here, 0:128] = v[:, 128:256]

    tail_qk = remote(qk.at[:, pl.ds(ROWS, CAP), :], qk.at[:, pl.ds(0, CAP), :], t_send.at[0], t_recv.at[0], to_after)
    tail_v = remote(
        vv.at[:, pl.ds(ROWS, CAP), pl.ds(0, 128)], vv.at[:, pl.ds(0, CAP), pl.ds(0, 128)],
        t_send.at[1], t_recv.at[1], to_after,
    )

    def arrive(i):
        gather_wait(0, i)
        gather_wait(1, i)
        gather_copy(2, i).start()
        gather_copy(3, i).start()

    def more(i):
        gather_copy(0, i).start()
        gather_copy(1, i).start()

    arrive(0)
    more(2)
    arrive(1)
    more(3)
    project(0)
    tail_qk.start()
    tail_v.start()
    arrive(2)
    project(1)

    lanes = lax.broadcasted_iota(jnp.int32, (1, 128), 1) < HS

    def attend(block, target, part=None, span=None):
        first, extent = bands[block] if span is None else span
        rows = slice(block * BLK, (block + 1) * BLK)
        span = slice(first, first + extent)

        def pair_step(pair, _):
            cols = pl.ds(pl.multiple_of(pair * 128, 128), 128)
            q = qk[0, rows, cols]
            for half in range(2):
                q_half = jnp.where(lanes if half == 0 else ~lanes, q, jnp.zeros_like(q))
                for k in range(0, extent, BLK):
                    score[half, :, k : k + BLK] = lax.dot_general(
                        q_half, qk[1, first + k : first + k + BLK, cols], (((1,), (1,)), ((), ())),
                        preferred_element_type=F32,
                    )
            results = []
            for half in range(2):
                for r in range(0, BLK, TILE):
                    tile = slice(r, r + TILE)
                    allowed = score[half, tile, 0:extent] + bias[block * BLK + r : block * BLK + r + TILE, span]
                    top = jnp.max(allowed, axis=1, keepdims=True)
                    if part == 0:
                        top_held[pair, half, tile, :] = jnp.broadcast_to(top, (TILE, 128))
                    elif part == 1:
                        old = top_held[pair, half, tile, :]
                        top = jnp.maximum(old[:, 0:1], top)
                        shrink[half, tile, :] = jnp.exp2(old - top)
                    prob[half, tile, 0:extent] = jnp.exp2(allowed - top).astype(BF16)
                results.append(jnp.dot(prob[half, :, 0:extent], vv[pair, span, :], preferred_element_type=F32))
            total = jnp.where(lanes, results[0][:, 0:128], results[1][:, 0:128])
            weight = jnp.where(lanes, results[0][:, 128:256], results[1][:, 128:256])
            if part == 0:
                held[pair, 0] = total
                held[pair, 1] = weight
            else:
                if part == 1:
                    scale = jnp.where(lanes, shrink[0], shrink[1])
                    total = total + scale * held[pair, 0]
                    weight = weight + scale * held[pair, 1]
                target[:, cols] = (total / weight).astype(BF16)
            return 0

        lax.fori_loop(0, 2, pair_step, 0)

    attend(3, att, 0, (768, 512))
    arrive(3)
    project(2)
    project(3)
    load_wo.wait()
    give_back = remote(attin, back, b_send, b_recv, to_before)

    half = BLK // 2
    low, high = pl.ds(0, half), pl.ds(half, half)

    def rs_copy(kind, b):
        src, dst, there = (
            (part.at[b, far, low, :], hop.at[b, 0], to_right),
            (part.at[b, far, high, :], hop.at[b, 1], to_left),
            (part.at[b, right, high, :], fin.at[b, 0, high, :], to_right),
            (part.at[b, left, low, :], fin.at[b, 1, low, :], to_left),
            (relay.at[b, 0], fin.at[b, 0, low, :], to_right),
            (relay.at[b, 1], fin.at[b, 1, high, :], to_left),
        )[kind]
        return remote(src, dst, rs_send.at[kind, b], rs_recv.at[kind, b], there)

    def pass_on(b):
        rs_copy(0, b).wait_recv()
        relay[b, 0] = (hop[b, 0].astype(F32) + part[b, right, low, :].astype(F32)).astype(BF16)
        rs_copy(4, b).start()
        rs_copy(1, b).wait_recv()
        relay[b, 1] = (hop[b, 1].astype(F32) + part[b, left, high, :].astype(F32)).astype(BF16)
        rs_copy(5, b).start()

    order = (2, 1, 0, 3)
    for step, b in enumerate(order):
        if step == 0:
            attend(3, att, 1, (256, 512))
        elif step == 1:
            admit()
            tail_qk.wait_recv()
            tail_v.wait_recv()
            attend(2, att)
        elif step == 2:
            attend(0, attin)
            give_back.start()
            attend(1, att)
        else:
            attend(4, att)
            give_back.wait_recv()
            moved = labcol[ALL - BLK : ALL, :] < 0.0
            for cols in (slice(0, 128), slice(128, 256)):
                att[:, cols] = jnp.where(moved, back[:, cols].astype(F32), att[:, cols].astype(F32)).astype(BF16)
        rows = att[...]
        for p in range(PARTS):
            part[b, p] = jnp.dot(
                rows, wo[:, p * WIDTH : (p + 1) * WIDTH], preferred_element_type=F32
            ).astype(BF16)
        for kind in range(4):
            rs_copy(kind, b).start()
        if step >= 2:
            pass_on(order[step - 2])

    def store_out(b):
        rows = pl.ds(b * BLK, BLK)
        return pltpu.make_async_copy(outv.at[rows, :], out_any.at[rows, :], out_sem.at[b])

    def finish(b):
        for kind in range(2, 6):
            rs_copy(kind, b).wait_recv()
        rows = slice(b * BLK, (b + 1) * BLK)
        outv[rows, :] = (
            xg[me, rows, :].astype(F32)
            + part[b, me].astype(F32)
            + fin[b, 0].astype(F32)
            + fin[b, 1].astype(F32)
        ).astype(BF16)
        store_out(b).start()

    pass_on(order[2])
    finish(order[0])
    pass_on(order[3])
    finish(order[1])
    finish(order[2])
    finish(order[3])

    def drain(i, _):
        for kind in range(4):
            gather_copy(kind, i).wait_send()
        return 0

    lax.fori_loop(0, NCH, drain, 0)
    code.wait_send()
    tail_qk.wait_send()
    tail_v.wait_send()
    give_back.wait_send()
    for b in range(NBLK):
        for kind in range(6):
            rs_copy(kind, b).wait_send()
        store_out(b).wait()


def local(tokens, norm_gain, w_qkv, w_out, window_id, carry):
    there = pl.BlockSpec(memory_space=pltpu.HBM)
    dma = pltpu.SemaphoreType.DMA
    return pl.pallas_call(
        kernel,
        out_shape=jax.ShapeDtypeStruct(tokens.shape, BF16),
        in_specs=[there] * 5 + [pl.BlockSpec(memory_space=pltpu.SMEM)],
        out_specs=pl.BlockSpec(memory_space=pl.ANY),
        scratch_shapes=[
            pltpu.VMEM((1, PARTS * WIDTH), F32),
            pltpu.VMEM((1, ROWS), jnp.int32),
            pltpu.VMEM((PARTS, ROWS, WIDTH), BF16),
            pltpu.VMEM((3, PARTS * WIDTH, WIDTH), BF16),
            pltpu.VMEM((WIDTH, PARTS * WIDTH), BF16),
            pltpu.VMEM((CH, PARTS * WIDTH), BF16),
            pltpu.VMEM((2, ALL, WIDTH), BF16),
            pltpu.VMEM((2, ALL, WIDTH), BF16),
            pltpu.VMEM((8, 128), F32),
            pltpu.VMEM((8, 128), F32),
            pltpu.VMEM((ALL, ALL), F32),
            pltpu.VMEM((ALL, 128), F32),
            pltpu.VMEM((CAP, WIDTH), BF16),
            pltpu.VMEM((BLK, WIDTH), BF16),
            pltpu.VMEM((CAP, WIDTH), BF16),
            pltpu.VMEM((NBLK, PARTS, BLK, WIDTH), BF16),
            pltpu.VMEM((NBLK, 2, BLK // 2, WIDTH), BF16),
            pltpu.VMEM((NBLK, 2, BLK // 2, WIDTH), BF16),
            pltpu.VMEM((NBLK, 2, BLK, WIDTH), BF16),
            pltpu.VMEM((2, BLK, ALL), F32),
            pltpu.VMEM((2, BLK, ALL), BF16),
            pltpu.VMEM((ROWS, WIDTH), BF16),
            pltpu.VMEM((2, 2, BLK, 128), F32),
            pltpu.VMEM((2, 2, BLK, 128), F32),
            pltpu.VMEM((2, BLK, 128), F32),
            dma,
            dma((4,)),
            dma((4, NCH)),
            dma((4, NCH)),
            dma,
            dma,
            dma((2,)),
            dma((2,)),
            dma,
            dma,
            dma((6, NBLK)),
            dma((6, NBLK)),
            dma((NBLK,)),
        ],
        compiler_params=pltpu.CompilerParams(
            collective_id=0, has_side_effects=True, vmem_limit_bytes=56 * 1024 * 1024
        ),
        cost_estimate=pl.CostEstimate(flops=4_000_000_000, bytes_accessed=4_000_000, transcendentals=5_000_000),
    )(tokens, norm_gain.reshape(1, PARTS * WIDTH), w_qkv, w_out, window_id, carry)


def solution(mesh):
    return jax.shard_map(
        local,
        mesh=mesh,
        in_specs=(
            P("space", "head"),
            P(),
            P(None, None, "head"),
            P("head", None),
            P("space", None),
            P("space"),
        ),
        out_specs=P("space", "head"),
        check_vma=False,
    )
```

```python
import functools
import math

import jax
import jax.numpy as jnp
from jax import lax
from jax.experimental import pallas as pl
from jax.experimental.pallas import tpu as pltpu
from jax.sharding import PartitionSpec as P

MESH = pl.DeviceIdType.MESH
F32 = jnp.float32
BF16 = jnp.bfloat16

HS = 64
CAP = 256
ROWS = 1024
ALL = ROWS + CAP
WIDTH = 256
PARTS = 4
CH = 256
LANE = 128
NCH = ROWS // CH
BLK = 256
NBLK = ROWS // BLK
AHEAD = 2
TILE = 16
EPS = 1e-05
QSCALE = HS**-0.5 * math.log2(math.e)
NEG = -1e30


def chunk_at(i):
    return NCH - 1 - i


def kernel(
    tok_hbm, gain_hbm, wqkv_hbm, wout_hbm, wid_hbm, carry_ref, out_any,
    gain_ref, wid_ref, xg, wq, wo, normed, qk, vv, lab, labin, bias, labcol, back, att, attin, part, hop, relay, fin,
    score, prob, outv, held, top_held, shrink,
    own_sem, wsem, ag_send, ag_recv, c_send, c_recv, t_send, t_recv, b_send, b_recv,
    rs_send, rs_recv, out_sem,
):
    me = lax.axis_index("head")
    spot = lax.axis_index("space")
    spots = lax.axis_size("space")
    right, left = lax.rem(me + 1, PARTS), lax.rem(me + PARTS - 1, PARTS)
    far = lax.rem(me + 2, PARTS)
    after, before = lax.rem(spot + 1, spots), lax.rem(spot + spots - 1, spots)
    to_right, to_left = {"head": right}, {"head": left}
    to_after, to_before = {"space": after}, {"space": before}

    own = pltpu.make_async_copy(tok_hbm, xg.at[me], own_sem)
    own.start()

    barrier = pltpu.get_barrier_semaphore()
    for there in (to_right, to_left, to_before):
        pl.semaphore_signal(barrier, inc=1, device_id=there, device_id_type=MESH)

    load_wid = pltpu.make_async_copy(wid_hbm, wid_ref, wsem.at[2])
    load_wid.start()
    load_gain = pltpu.make_async_copy(gain_hbm, gain_ref, wsem.at[3])
    load_gain.start()
    load_wq = pltpu.make_async_copy(wqkv_hbm, wq, wsem.at[0])
    load_wq.start()
    load_wo = pltpu.make_async_copy(wout_hbm, wo, wsem.at[1])
    load_wo.start()

    count = carry_ref[0]
    lab[...] = jnp.full(lab.shape, count, jnp.int32).astype(F32)
    own.wait()
    pl.semaphore_wait(barrier, 3)

    def remote(src, dst, send, recv, there):
        return pltpu.make_async_remote_copy(
            src_ref=src, dst_ref=dst, send_sem=send, recv_sem=recv, device_id=there, device_id_type=MESH
        )

    def gather_copy(kind, i):
        rows = chunk_at(i) * CH
        slot, start, size, there = (
            (me, rows, CH, to_right),
            (me, rows, CH, to_left),
            (left, rows, CH // 2, to_right),
            (right, rows + CH // 2, CH // 2, to_left),
        )[kind]
        view = xg.at[slot, pl.ds(pl.multiple_of(start, CH // 2), size), :]
        return remote(view, view, ag_send.at[kind, i], ag_recv.at[kind, i], there)

    def gather_wait(kind, i):
        rows = chunk_at(i) * CH
        slot, start, size = (
            (left, rows, CH),
            (right, rows, CH),
            (far, rows, CH // 2),
            (far, rows + CH // 2, CH // 2),
        )[kind]
        view = xg.at[slot, pl.ds(pl.multiple_of(start, CH // 2), size), :]
        remote(view, view, ag_send.at[kind, i], ag_recv.at[kind, i], to_right).wait_recv()

    for i in range(AHEAD):
        gather_copy(0, i).start()
        gather_copy(1, i).start()
    code = remote(lab, labin, c_send, c_recv, to_after)
    code.start()

    vv[:, :, LANE:] = jnp.ones((2, ALL, LANE), BF16)

    def columns_of(queries, first):
        for k in range(queries.shape[1] // LANE):
            piece = jnp.broadcast_to(queries[0:1, k * LANE : (k + 1) * LANE], (LANE, LANE))
            labcol[first + k * LANE : first + (k + 1) * LANE, :] = piece.T

    def allow(block, queries, first, start, stop):
        keys = jnp.where(queries < 0.0, -2.0, queries)
        rows = slice(block * BLK, (block + 1) * BLK)
        column = labcol[rows, :]
        for k in range(start, stop, LANE):
            bias[rows, k : k + LANE] = jnp.where(column == keys[0:1, k - first : k - first + LANE], 0.0, NEG)

    def labels_here():
        spread = jnp.broadcast_to(wid_ref[...].astype(F32), (8, ROWS))
        place = lax.broadcasted_iota(jnp.int32, (8, ROWS), 1)
        return jnp.where(place >= ROWS - count, -1.0, spread)

    bands = {0: (0, 768), 1: (0, 1024), 2: (0, 1280), 3: (256, 1024), 4: (512, 768)}
    load_wid.wait()
    mine = labels_here()
    columns_of(mine, CAP)
    for block in range(1, NBLK + 1):
        first, extent = bands[block]
        allow(block, mine, CAP, max(first, CAP), first + extent)

    def admit():
        code.wait_recv()
        place = lax.broadcasted_iota(jnp.int32, (8, CAP), 1).astype(F32)
        theirs = jnp.where(place >= CAP - labin[0:1, 0:1], 0.0, -1.0)
        columns_of(theirs, 0)
        for block in range(3):
            allow(block, theirs, 0, 0, CAP)
        allow(0, labels_here(), CAP, CAP, 768)

    load_gain.wait()
    load_wq.wait()
    gain = gain_ref[...]

    def project(i):
        gather_wait(2, i)
        gather_wait(3, i)
        rows = pl.multiple_of(chunk_at(i) * CH, CH)
        for r in range(0, CH, TILE):
            slices = [
                xg[p, pl.ds(pl.multiple_of(rows + r, TILE), TILE), :].astype(F32) for p in range(PARTS)
            ]
            mean = jnp.sum(sum(slices), axis=1, keepdims=True) * (1.0 / (PARTS * WIDTH))
            centred = [x - mean for x in slices]
            var = jnp.sum(sum(x * x for x in centred), axis=1, keepdims=True) * (1.0 / (PARTS * WIDTH))
            rstd = lax.rsqrt(var + EPS)
            for p in range(PARTS):
                cols = slice(p * WIDTH, (p + 1) * WIDTH)
                normed[r : r + TILE, cols] = (centred[p] * rstd * gain[:, cols]).astype(BF16)
        here = pl.ds(pl.multiple_of(rows + CAP, CH), CH)
        x = normed[...]
        qk[0, here, :] = (jnp.dot(x, wq[0], preferred_element_type=F32) * QSCALE).astype(BF16)
        qk[1, here, :] = jnp.dot(x, wq[1], preferred_element_type=F32).astype(BF16)
        v = jnp.dot(x, wq[2], preferred_element_type=F32).astype(BF16)
        vv[0, here, 0:128] = v[:, 0:128]
        vv[1, here, 0:128] = v[:, 128:256]

    tail_qk = remote(qk.at[:, pl.ds(ROWS, CAP), :], qk.at[:, pl.ds(0, CAP), :], t_send.at[0], t_recv.at[0], to_after)
    tail_v = remote(
        vv.at[:, pl.ds(ROWS, CAP), pl.ds(0, 128)], vv.at[:, pl.ds(0, CAP), pl.ds(0, 128)],
        t_send.at[1], t_recv.at[1], to_after,
    )

    def arrive(i):
        gather_wait(0, i)
        gather_wait(1, i)
        gather_copy(2, i).start()
        gather_copy(3, i).start()

    def more(i):
        gather_copy(0, i).start()
        gather_copy(1, i).start()

    arrive(0)
    more(2)
    arrive(1)
    more(3)
    project(0)
    tail_qk.start()
    tail_v.start()
    arrive(2)
    project(1)

    lanes = lax.broadcasted_iota(jnp.int32, (1, 128), 1) < HS

    def attend(block, target, part=None, span=None):
        first, extent = bands[block] if span is None else span
        rows = slice(block * BLK, (block + 1) * BLK)
        span = slice(first, first + extent)

        def pair_step(pair, _):
            cols = pl.ds(pl.multiple_of(pair * 128, 128), 128)
            q = qk[0, rows, cols]
            for half in range(2):
                q_half = jnp.where(lanes if half == 0 else ~lanes, q, jnp.zeros_like(q))
                for k in range(0, extent, BLK):
                    score[half, :, k : k + BLK] = lax.dot_general(
                        q_half, qk[1, first + k : first + k + BLK, cols], (((1,), (1,)), ((), ())),
                        preferred_element_type=F32,
                    )
            results = []
            for half in range(2):
                for r in range(0, BLK, TILE):
                    tile = slice(r, r + TILE)
                    allowed = score[half, tile, 0:extent] + bias[block * BLK + r : block * BLK + r + TILE, span]
                    top = jnp.max(allowed, axis=1, keepdims=True)
                    if part == 0:
                        top_held[pair, half, tile, :] = jnp.broadcast_to(top, (TILE, 128))
                    elif part == 1:
                        old = top_held[pair, half, tile, :]
                        top = jnp.maximum(old[:, 0:1], top)
                        shrink[half, tile, :] = jnp.exp2(old - top)
                    prob[half, tile, 0:extent] = jnp.exp2(allowed - top).astype(BF16)
                results.append(jnp.dot(prob[half, :, 0:extent], vv[pair, span, :], preferred_element_type=F32))
            total = jnp.where(lanes, results[0][:, 0:128], results[1][:, 0:128])
            weight = jnp.where(lanes, results[0][:, 128:256], results[1][:, 128:256])
            if part == 0:
                held[pair, 0] = total
                held[pair, 1] = weight
            else:
                if part == 1:
                    scale = jnp.where(lanes, shrink[0], shrink[1])
                    total = total + scale * held[pair, 0]
                    weight = weight + scale * held[pair, 1]
                target[:, cols] = (total / weight).astype(BF16)
            return 0

        lax.fori_loop(0, 2, pair_step, 0)

    attend(3, att, 0, (768, 512))
    arrive(3)
    project(2)
    project(3)
    load_wo.wait()
    give_back = remote(attin, back, b_send, b_recv, to_before)

    half = BLK // 2
    low, high = pl.ds(0, half), pl.ds(half, half)

    def rs_copy(kind, b):
        src, dst, there = (
            (part.at[b, far, low, :], hop.at[b, 0], to_right),
            (part.at[b, far, high, :], hop.at[b, 1], to_left),
            (part.at[b, right, high, :], fin.at[b, 0, high, :], to_right),
            (part.at[b, left, low, :], fin.at[b, 1, low, :], to_left),
            (relay.at[b, 0], fin.at[b, 0, low, :], to_right),
            (relay.at[b, 1], fin.at[b, 1, high, :], to_left),
        )[kind]
        return remote(src, dst, rs_send.at[kind, b], rs_recv.at[kind, b], there)

    def pass_on(b):
        rs_copy(0, b).wait_recv()
        relay[b, 0] = (hop[b, 0].astype(F32) + part[b, right, low, :].astype(F32)).astype(BF16)
        rs_copy(4, b).start()
        rs_copy(1, b).wait_recv()
        relay[b, 1] = (hop[b, 1].astype(F32) + part[b, left, high, :].astype(F32)).astype(BF16)
        rs_copy(5, b).start()

    order = (2, 1, 0, 3)
    for step, b in enumerate(order):
        if step == 0:
            attend(3, att, 1, (256, 512))
        elif step == 1:
            admit()
            tail_qk.wait_recv()
            tail_v.wait_recv()
            attend(2, att)
        elif step == 2:
            attend(0, attin)
            give_back.start()
            pass_on(order[1])
            attend(1, att)
        else:
            attend(4, att)
            pass_on(order[2])
            give_back.wait_recv()
            moved = labcol[ALL - BLK : ALL, :] < 0.0
            for cols in (slice(0, 128), slice(128, 256)):
                att[:, cols] = jnp.where(moved, back[:, cols].astype(F32), att[:, cols].astype(F32)).astype(BF16)
        rows = att[...]
        for p in range(PARTS):
            part[b, p] = jnp.dot(
                rows, wo[:, p * WIDTH : (p + 1) * WIDTH], preferred_element_type=F32
            ).astype(BF16)
        for kind in range(4):
            rs_copy(kind, b).start()
        if step == 1:
            pass_on(order[0])

    def store_out(b):
        rows = pl.ds(b * BLK, BLK)
        return pltpu.make_async_copy(outv.at[rows, :], out_any.at[rows, :], out_sem.at[b])

    def finish(b):
        for kind in range(2, 6):
            rs_copy(kind, b).wait_recv()
        rows = slice(b * BLK, (b + 1) * BLK)
        outv[rows, :] = (
            xg[me, rows, :].astype(F32)
            + part[b, me].astype(F32)
            + fin[b, 0].astype(F32)
            + fin[b, 1].astype(F32)
        ).astype(BF16)
        store_out(b).start()

    finish(order[0])
    pass_on(order[3])
    finish(order[1])
    finish(order[2])
    finish(order[3])

    def drain(i, _):
        for kind in range(4):
            gather_copy(kind, i).wait_send()
        return 0

    lax.fori_loop(0, NCH, drain, 0)
    code.wait_send()
    tail_qk.wait_send()
    tail_v.wait_send()
    give_back.wait_send()
    for b in range(NBLK):
        for kind in range(6):
            rs_copy(kind, b).wait_send()
        store_out(b).wait()


def local(tokens, norm_gain, w_qkv, w_out, window_id, carry):
    there = pl.BlockSpec(memory_space=pltpu.HBM)
    dma = pltpu.SemaphoreType.DMA
    return pl.pallas_call(
        kernel,
        out_shape=jax.ShapeDtypeStruct(tokens.shape, BF16),
        in_specs=[there] * 5 + [pl.BlockSpec(memory_space=pltpu.SMEM)],
        out_specs=pl.BlockSpec(memory_space=pl.ANY),
        scratch_shapes=[
            pltpu.VMEM((1, PARTS * WIDTH), F32),
            pltpu.VMEM((1, ROWS), jnp.int32),
            pltpu.VMEM((PARTS, ROWS, WIDTH), BF16),
            pltpu.VMEM((3, PARTS * WIDTH, WIDTH), BF16),
            pltpu.VMEM((WIDTH, PARTS * WIDTH), BF16),
            pltpu.VMEM((CH, PARTS * WIDTH), BF16),
            pltpu.VMEM((2, ALL, WIDTH), BF16),
            pltpu.VMEM((2, ALL, WIDTH), BF16),
            pltpu.VMEM((8, 128), F32),
            pltpu.VMEM((8, 128), F32),
            pltpu.VMEM((ALL, ALL), F32),
            pltpu.VMEM((ALL, 128), F32),
            pltpu.VMEM((CAP, WIDTH), BF16),
            pltpu.VMEM((BLK, WIDTH), BF16),
            pltpu.VMEM((CAP, WIDTH), BF16),
            pltpu.VMEM((NBLK, PARTS, BLK, WIDTH), BF16),
            pltpu.VMEM((NBLK, 2, BLK // 2, WIDTH), BF16),
            pltpu.VMEM((NBLK, 2, BLK // 2, WIDTH), BF16),
            pltpu.VMEM((NBLK, 2, BLK, WIDTH), BF16),
            pltpu.VMEM((2, BLK, ALL), F32),
            pltpu.VMEM((2, BLK, ALL), BF16),
            pltpu.VMEM((ROWS, WIDTH), BF16),
            pltpu.VMEM((2, 2, BLK, 128), F32),
            pltpu.VMEM((2, 2, BLK, 128), F32),
            pltpu.VMEM((2, BLK, 128), F32),
            dma,
            dma((4,)),
            dma((4, NCH)),
            dma((4, NCH)),
            dma,
            dma,
            dma((2,)),
            dma((2,)),
            dma,
            dma,
            dma((6, NBLK)),
            dma((6, NBLK)),
            dma((NBLK,)),
        ],
        compiler_params=pltpu.CompilerParams(
            collective_id=0, has_side_effects=True, vmem_limit_bytes=56 * 1024 * 1024
        ),
        cost_estimate=pl.CostEstimate(flops=4_000_000_000, bytes_accessed=4_000_000, transcendentals=5_000_000),
    )(tokens, norm_gain.reshape(1, PARTS * WIDTH), w_qkv, w_out, window_id, carry)


def solution(mesh):
    return jax.shard_map(
        local,
        mesh=mesh,
        in_specs=(
            P("space", "head"),
            P(),
            P(None, None, "head"),
            P("head", None),
            P("space", None),
            P("space"),
        ),
        out_specs=P("space", "head"),
        check_vma=False,
    )
```

```python
import functools
import math

import jax
import jax.numpy as jnp
from jax import lax
from jax.experimental import pallas as pl
from jax.experimental.pallas import tpu as pltpu
from jax.sharding import PartitionSpec as P

MESH = pl.DeviceIdType.MESH
F32 = jnp.float32
BF16 = jnp.bfloat16

HS = 64
CAP = 256
ROWS = 1024
ALL = ROWS + CAP
WIDTH = 256
PARTS = 4
CH = 256
LANE = 128
NCH = ROWS // CH
BLK = 256
NBLK = ROWS // BLK
AHEAD = 2
TILE = 16
EPS = 1e-05
QSCALE = HS**-0.5 * math.log2(math.e)
NEG = -1e30


def chunk_at(i):
    return NCH - 1 - i


def kernel(
    tok_hbm, gain_hbm, wqkv_hbm, wout_hbm, wid_hbm, carry_ref, out_any,
    gain_ref, wid_ref, xg, wq, wo, normed, qk, vv, lab, labin, bias, labcol, back, att, attin, part, hop, relay, fin,
    score, prob, outv, held, top_held, shrink,
    own_sem, wsem, ag_send, ag_recv, c_send, c_recv, t_send, t_recv, b_send, b_recv,
    rs_send, rs_recv, out_sem,
):
    me = lax.axis_index("head")
    spot = lax.axis_index("space")
    spots = lax.axis_size("space")
    right, left = lax.rem(me + 1, PARTS), lax.rem(me + PARTS - 1, PARTS)
    far = lax.rem(me + 2, PARTS)
    after, before = lax.rem(spot + 1, spots), lax.rem(spot + spots - 1, spots)
    to_right, to_left = {"head": right}, {"head": left}
    to_after, to_before = {"space": after}, {"space": before}

    own = pltpu.make_async_copy(tok_hbm, xg.at[me], own_sem)
    own.start()

    barrier = pltpu.get_barrier_semaphore()
    for there in (to_right, to_left, to_before):
        pl.semaphore_signal(barrier, inc=1, device_id=there, device_id_type=MESH)

    load_wid = pltpu.make_async_copy(wid_hbm, wid_ref, wsem.at[2])
    load_wid.start()
    load_gain = pltpu.make_async_copy(gain_hbm, gain_ref, wsem.at[3])
    load_gain.start()
    load_wq = pltpu.make_async_copy(wqkv_hbm, wq, wsem.at[0])
    load_wq.start()
    load_wo = pltpu.make_async_copy(wout_hbm, wo, wsem.at[1])
    load_wo.start()

    count = carry_ref[0]
    lab[...] = jnp.full(lab.shape, count, jnp.int32).astype(F32)
    own.wait()
    pl.semaphore_wait(barrier, 3)

    def remote(src, dst, send, recv, there):
        return pltpu.make_async_remote_copy(
            src_ref=src, dst_ref=dst, send_sem=send, recv_sem=recv, device_id=there, device_id_type=MESH
        )

    def gather_copy(kind, i):
        rows = chunk_at(i) * CH
        slot, start, size, there = (
            (me, rows, CH, to_right),
            (me, rows, CH, to_left),
            (left, rows, CH // 2, to_right),
            (right, rows + CH // 2, CH // 2, to_left),
        )[kind]
        view = xg.at[slot, pl.ds(pl.multiple_of(start, CH // 2), size), :]
        return remote(view, view, ag_send.at[kind, i], ag_recv.at[kind, i], there)

    def gather_wait(kind, i):
        rows = chunk_at(i) * CH
        slot, start, size = (
            (left, rows, CH),
            (right, rows, CH),
            (far, rows, CH // 2),
            (far, rows + CH // 2, CH // 2),
        )[kind]
        view = xg.at[slot, pl.ds(pl.multiple_of(start, CH // 2), size), :]
        remote(view, view, ag_send.at[kind, i], ag_recv.at[kind, i], to_right).wait_recv()

    for i in range(AHEAD):
        gather_copy(0, i).start()
        gather_copy(1, i).start()
    code = remote(lab, labin, c_send, c_recv, to_after)
    code.start()

    vv[:, :, LANE:] = jnp.ones((2, ALL, LANE), BF16)

    def columns_of(queries, first):
        for k in range(queries.shape[1] // LANE):
            piece = jnp.broadcast_to(queries[0:1, k * LANE : (k + 1) * LANE], (LANE, LANE))
            labcol[first + k * LANE : first + (k + 1) * LANE, :] = piece.T

    def allow(block, queries, first, start, stop):
        keys = jnp.where(queries < 0.0, -2.0, queries)
        rows = slice(block * BLK, (block + 1) * BLK)
        column = labcol[rows, :]
        for k in range(start, stop, LANE):
            bias[rows, k : k + LANE] = jnp.where(column == keys[0:1, k - first : k - first + LANE], 0.0, NEG)

    def labels_here():
        spread = jnp.broadcast_to(wid_ref[...].astype(F32), (8, ROWS))
        place = lax.broadcasted_iota(jnp.int32, (8, ROWS), 1)
        return jnp.where(place >= ROWS - count, -1.0, spread)

    bands = {0: (0, 768), 1: (0, 1024), 2: (0, 1280), 3: (256, 1024), 4: (512, 768)}
    load_wid.wait()
    mine = labels_here()
    columns_of(mine, CAP)
    for block in range(1, NBLK + 1):
        first, extent = bands[block]
        allow(block, mine, CAP, max(first, CAP), first + extent)

    def admit():
        code.wait_recv()
        place = lax.broadcasted_iota(jnp.int32, (8, CAP), 1).astype(F32)
        theirs = jnp.where(place >= CAP - labin[0:1, 0:1], 0.0, -1.0)
        columns_of(theirs, 0)
        for block in range(3):
            allow(block, theirs, 0, 0, CAP)
        allow(0, labels_here(), CAP, CAP, 768)

    load_gain.wait()
    load_wq.wait()
    gain = gain_ref[...]

    def project(i):
        gather_wait(2, i)
        gather_wait(3, i)
        rows = pl.multiple_of(chunk_at(i) * CH, CH)
        for r in range(0, CH, TILE):
            slices = [
                xg[p, pl.ds(pl.multiple_of(rows + r, TILE), TILE), :].astype(F32) for p in range(PARTS)
            ]
            mean = jnp.sum(sum(slices), axis=1, keepdims=True) * (1.0 / (PARTS * WIDTH))
            centred = [x - mean for x in slices]
            var = jnp.sum(sum(x * x for x in centred), axis=1, keepdims=True) * (1.0 / (PARTS * WIDTH))
            rstd = lax.rsqrt(var + EPS)
            for p in range(PARTS):
                cols = slice(p * WIDTH, (p + 1) * WIDTH)
                normed[r : r + TILE, cols] = (centred[p] * rstd * gain[:, cols]).astype(BF16)
        here = pl.ds(pl.multiple_of(rows + CAP, CH), CH)
        x = normed[...]
        qk[0, here, :] = (jnp.dot(x, wq[0], preferred_element_type=F32) * QSCALE).astype(BF16)
        qk[1, here, :] = jnp.dot(x, wq[1], preferred_element_type=F32).astype(BF16)
        v = jnp.dot(x, wq[2], preferred_element_type=F32).astype(BF16)
        vv[0, here, 0:128] = v[:, 0:128]
        vv[1, here, 0:128] = v[:, 128:256]

    tail_qk = remote(qk.at[:, pl.ds(ROWS, CAP), :], qk.at[:, pl.ds(0, CAP), :], t_send.at[0], t_recv.at[0], to_after)
    tail_v = remote(
        vv.at[:, pl.ds(ROWS, CAP), pl.ds(0, 128)], vv.at[:, pl.ds(0, CAP), pl.ds(0, 128)],
        t_send.at[1], t_recv.at[1], to_after,
    )

    def arrive(i):
        gather_wait(0, i)
        gather_wait(1, i)
        gather_copy(2, i).start()
        gather_copy(3, i).start()

    def more(i):
        gather_copy(0, i).start()
        gather_copy(1, i).start()

    arrive(0)
    more(2)
    arrive(1)
    more(3)
    project(0)
    tail_qk.start()
    tail_v.start()
    arrive(2)
    project(1)
    arrive(3)

    lanes = lax.broadcasted_iota(jnp.int32, (1, 128), 1) < HS

    def attend(block, target, part=None, span=None):
        first, extent = bands[block] if span is None else span
        rows = slice(block * BLK, (block + 1) * BLK)
        span = slice(first, first + extent)

        def pair_step(pair, _):
            cols = pl.ds(pl.multiple_of(pair * 128, 128), 128)
            q = qk[0, rows, cols]
            for half in range(2):
                q_half = jnp.where(lanes if half == 0 else ~lanes, q, jnp.zeros_like(q))
                for k in range(0, extent, BLK):
                    score[half, :, k : k + BLK] = lax.dot_general(
                        q_half, qk[1, first + k : first + k + BLK, cols], (((1,), (1,)), ((), ())),
                        preferred_element_type=F32,
                    )
            results = []
            for half in range(2):
                for r in range(0, BLK, TILE):
                    tile = slice(r, r + TILE)
                    allowed = score[half, tile, 0:extent] + bias[block * BLK + r : block * BLK + r + TILE, span]
                    top = jnp.max(allowed, axis=1, keepdims=True)
                    if part == 0:
                        top_held[pair, half, tile, :] = jnp.broadcast_to(top, (TILE, 128))
                    elif part == 1:
                        old = top_held[pair, half, tile, :]
                        top = jnp.maximum(old[:, 0:1], top)
                        shrink[half, tile, :] = jnp.exp2(old - top)
                    prob[half, tile, 0:extent] = jnp.exp2(allowed - top).astype(BF16)
                results.append(jnp.dot(prob[half, :, 0:extent], vv[pair, span, :], preferred_element_type=F32))
            total = jnp.where(lanes, results[0][:, 0:128], results[1][:, 0:128])
            weight = jnp.where(lanes, results[0][:, 128:256], results[1][:, 128:256])
            if part == 0:
                held[pair, 0] = total
                held[pair, 1] = weight
            else:
                if part == 1:
                    scale = jnp.where(lanes, shrink[0], shrink[1])
                    total = total + scale * held[pair, 0]
                    weight = weight + scale * held[pair, 1]
                target[:, cols] = (total / weight).astype(BF16)
            return 0

        lax.fori_loop(0, 2, pair_step, 0)

    project(2)
    attend(3, att, 0, (512, 768))
    project(3)
    load_wo.wait()
    give_back = remote(attin, back, b_send, b_recv, to_before)

    half = BLK // 2
    low, high = pl.ds(0, half), pl.ds(half, half)

    def rs_copy(kind, b):
        src, dst, there = (
            (part.at[b, far, low, :], hop.at[b, 0], to_right),
            (part.at[b, far, high, :], hop.at[b, 1], to_left),
            (part.at[b, right, high, :], fin.at[b, 0, high, :], to_right),
            (part.at[b, left, low, :], fin.at[b, 1, low, :], to_left),
            (relay.at[b, 0], fin.at[b, 0, low, :], to_right),
            (relay.at[b, 1], fin.at[b, 1, high, :], to_left),
        )[kind]
        return remote(src, dst, rs_send.at[kind, b], rs_recv.at[kind, b], there)

    def pass_on(b):
        rs_copy(0, b).wait_recv()
        relay[b, 0] = (hop[b, 0].astype(F32) + part[b, right, low, :].astype(F32)).astype(BF16)
        rs_copy(4, b).start()
        rs_copy(1, b).wait_recv()
        relay[b, 1] = (hop[b, 1].astype(F32) + part[b, left, high, :].astype(F32)).astype(BF16)
        rs_copy(5, b).start()

    order = (2, 1, 0, 3)
    for step, b in enumerate(order):
        if step == 0:
            attend(3, att, 1, (256, 256))
        elif step == 1:
            admit()
            tail_qk.wait_recv()
            tail_v.wait_recv()
            attend(2, att)
        elif step == 2:
            attend(0, attin)
            give_back.start()
            attend(1, att)
        else:
            attend(4, att)
            give_back.wait_recv()
            moved = labcol[ALL - BLK : ALL, :] < 0.0
            for cols in (slice(0, 128), slice(128, 256)):
                att[:, cols] = jnp.where(moved, back[:, cols].astype(F32), att[:, cols].astype(F32)).astype(BF16)
        rows = att[...]
        for p in range(PARTS):
            part[b, p] = jnp.dot(
                rows, wo[:, p * WIDTH : (p + 1) * WIDTH], preferred_element_type=F32
            ).astype(BF16)
        for kind in (0, 1):
            rs_copy(kind, b).start()
        if step >= 1:
            pass_on(order[step - 1])
        for kind in (2, 3):
            rs_copy(kind, b).start()

    def store_out(b):
        rows = pl.ds(b * BLK, BLK)
        return pltpu.make_async_copy(outv.at[rows, :], out_any.at[rows, :], out_sem.at[b])

    def finish(b):
        for kind in range(2, 6):
            rs_copy(kind, b).wait_recv()
        rows = slice(b * BLK, (b + 1) * BLK)
        outv[rows, :] = (
            xg[me, rows, :].astype(F32)
            + part[b, me].astype(F32)
            + fin[b, 0].astype(F32)
            + fin[b, 1].astype(F32)
        ).astype(BF16)
        store_out(b).start()

    finish(order[0])
    pass_on(order[3])
    finish(order[1])
    finish(order[2])
    finish(order[3])

    def drain(i, _):
        for kind in range(4):
            gather_copy(kind, i).wait_send()
        return 0

    lax.fori_loop(0, NCH, drain, 0)
    code.wait_send()
    tail_qk.wait_send()
    tail_v.wait_send()
    give_back.wait_send()
    for b in range(NBLK):
        for kind in range(6):
            rs_copy(kind, b).wait_send()
        store_out(b).wait()


def local(tokens, norm_gain, w_qkv, w_out, window_id, carry):
    there = pl.BlockSpec(memory_space=pltpu.HBM)
    dma = pltpu.SemaphoreType.DMA
    return pl.pallas_call(
        kernel,
        out_shape=jax.ShapeDtypeStruct(tokens.shape, BF16),
        in_specs=[there] * 5 + [pl.BlockSpec(memory_space=pltpu.SMEM)],
        out_specs=pl.BlockSpec(memory_space=pl.ANY),
        scratch_shapes=[
            pltpu.VMEM((1, PARTS * WIDTH), F32),
            pltpu.VMEM((1, ROWS), jnp.int32),
            pltpu.VMEM((PARTS, ROWS, WIDTH), BF16),
            pltpu.VMEM((3, PARTS * WIDTH, WIDTH), BF16),
            pltpu.VMEM((WIDTH, PARTS * WIDTH), BF16),
            pltpu.VMEM((CH, PARTS * WIDTH), BF16),
            pltpu.VMEM((2, ALL, WIDTH), BF16),
            pltpu.VMEM((2, ALL, WIDTH), BF16),
            pltpu.VMEM((8, 128), F32),
            pltpu.VMEM((8, 128), F32),
            pltpu.VMEM((ALL, ALL), F32),
            pltpu.VMEM((ALL, 128), F32),
            pltpu.VMEM((CAP, WIDTH), BF16),
            pltpu.VMEM((BLK, WIDTH), BF16),
            pltpu.VMEM((CAP, WIDTH), BF16),
            pltpu.VMEM((NBLK, PARTS, BLK, WIDTH), BF16),
            pltpu.VMEM((NBLK, 2, BLK // 2, WIDTH), BF16),
            pltpu.VMEM((NBLK, 2, BLK // 2, WIDTH), BF16),
            pltpu.VMEM((NBLK, 2, BLK, WIDTH), BF16),
            pltpu.VMEM((2, BLK, ALL), F32),
            pltpu.VMEM((2, BLK, ALL), BF16),
            pltpu.VMEM((ROWS, WIDTH), BF16),
            pltpu.VMEM((2, 2, BLK, 128), F32),
            pltpu.VMEM((2, 2, BLK, 128), F32),
            pltpu.VMEM((2, BLK, 128), F32),
            dma,
            dma((4,)),
            dma((4, NCH)),
            dma((4, NCH)),
            dma,
            dma,
            dma((2,)),
            dma((2,)),
            dma,
            dma,
            dma((6, NBLK)),
            dma((6, NBLK)),
            dma((NBLK,)),
        ],
        compiler_params=pltpu.CompilerParams(
            collective_id=0, has_side_effects=True, vmem_limit_bytes=56 * 1024 * 1024
        ),
        cost_estimate=pl.CostEstimate(flops=4_000_000_000, bytes_accessed=4_000_000, transcendentals=5_000_000),
    )(tokens, norm_gain.reshape(1, PARTS * WIDTH), w_qkv, w_out, window_id, carry)


def solution(mesh):
    return jax.shard_map(
        local,
        mesh=mesh,
        in_specs=(
            P("space", "head"),
            P(),
            P(None, None, "head"),
            P("head", None),
            P("space", None),
            P("space"),
        ),
        out_specs=P("space", "head"),
        check_vma=False,
    )
```
